32 devices in a mesh: groups: 2 (over y), dom: 4 (over z), probe: 2 (over x), orb: 2 (over core).
Axes of the slice: x: 2, y: 2, z: 4, core: 2. Of those that a mesh axis runs over, the one named last changes fastest.
Arguments:
- probes: float32 [1024, 16, 256], P(('groups', 'dom', 'orb'), None, 'probe'), parts along dimension 0, may hold values from -6 to 6
- blocks: bfloat16 [20480, 16, 16], P(('groups', 'dom', 'orb')), parts along dimension 0, may hold values from -0.0625 to 0.0625
- block_rows: int32 [20480], P(('groups', 'dom', 'orb')), parts along dimension 0, may hold values from 0 to 63
- block_cols: int32 [20480], P(('groups', 'dom', 'orb')), parts along dimension 0, may hold values from 0 to 95
- counts: int32 [16], P(('groups', 'dom', 'orb')), parts along dimension 0, may hold values from 640 to 1280, as said below
Outputs:
- last_vector: float32 [1024, 16, 256], P(('groups', 'dom', 'orb'), None, 'probe'), parts along dimension 0
- moments: float32 [18, 256], P('groups', 'probe'), parts along dimension 0
The draws below stay inside these ranges and needn't reach their ends.
There are 2 independent parts, one for each index of `groups`. The reference program is written for one: setup_inputs(seed, part) draws one part's arguments, and reference() takes and returns one part's arrays. A program takes and returns all parts, laid end to end along the dimension named above; each array names one. Nothing has to cross between parts.
Inputs may be any that keep to these rules, and one draw needn't show every extreme that they name: `counts`: some domain uses all 1280 slots in every draw.
All inputs are finite; a program needn't handle non-finite values.
Results may differ from the reference program's by a relative error of at most 0.0085.
Values may be sent and summed in bfloat16 or wider, within the bound.
No kernel may reach another device: no remote copies, remote signals or barrier semaphores. Data moves between devices by JAX's collectives and lax.ppermute only.
A program may use at most 192 MiB of HBM per device.

```python
import jax
import jax.numpy as jnp

ORB = 16
PROBES = 256
ATOMS_DEV = 64
BLK_PER = 20
STEPS = 8
HALO = 32
BLK_DEV = 1280
DOMAINS = 8
ATOMS = 512


def draw_counts(key, part):
    key = jax.random.fold_in(key, 5)
    values = jax.random.randint(key, (DOMAINS,), BLK_DEV // 2, BLK_DEV + 1)
    chosen = jax.random.randint(jax.random.fold_in(key, 1), (), 0, DOMAINS)
    return jnp.where(jnp.arange(DOMAINS) == chosen, BLK_DEV, values).astype(jnp.int32)


def set_ends(drawn, stream_key, smallest, high):
    longest = drawn.shape.index(max(drawn.shape))
    spots = []
    for shift in (0, 1):
        where = [jax.random.randint(jax.random.fold_in(stream_key, axis), (), 0, length) for axis, length in enumerate(drawn.shape)]
        where[longest] = (where[longest] + shift) % drawn.shape[longest]
        spots.append(tuple(where))
    return drawn.at[spots[0]].set(smallest).at[spots[1]].set(high)


def block_levels(stream_key, shape, cuts, smallest, high):
    def one(dim, parts):
        draws = jax.random.uniform(jax.random.fold_in(jax.random.fold_in(stream_key, 6), dim), (parts,), jnp.float32, smallest / len(cuts), high / len(cuts))
        return jnp.repeat(jnp.exp(draws), shape[dim] // parts).reshape((-1,) + (1,) * (len(shape) - dim - 1))

    level = one(*cuts[0])
    for cut in cuts[1:]:
        level = level * one(*cut)
    return level


def scatter_about(stream_key, dims, scale, bound, pieces=(), held_as=jnp.bfloat16):
    values = scale * jax.random.normal(stream_key, dims, jnp.float32)
    if pieces:
        values = values * block_levels(stream_key, dims, pieces, -0.22, 0.18)
    return jnp.clip(values, -bound, bound).astype(held_as)


def setup_inputs(seed: int = 0, part: int = 0) -> dict:
    splits = jax.random.split(jax.random.key(seed), 6)
    part_keys = jax.random.split(jax.random.fold_in(splits[5], part), 6)
    return {
        "probes": scatter_about(part_keys[0], (ATOMS, ORB, PROBES), 1.0, 6.0, ((0, 8), (2, 2)), jnp.float32),
        "blocks": scatter_about(part_keys[1], (DOMAINS * BLK_DEV, ORB, ORB), (2 * BLK_PER * ORB * ORB) ** -0.5, 0.0625, ((0, 8),)),
        "block_rows": set_ends(jax.random.randint(part_keys[2], (DOMAINS * BLK_DEV,), 0, ATOMS_DEV), jax.random.fold_in(part_keys[2], 1), 0, ATOMS_DEV - 1).astype(jnp.int32),
        "block_cols": set_ends(jax.random.randint(part_keys[3], (DOMAINS * BLK_DEV,), 0, ATOMS_DEV + HALO), jax.random.fold_in(part_keys[3], 1), 0, (ATOMS_DEV + HALO) - 1).astype(jnp.int32),
        "counts": draw_counts(jax.random.fold_in(jax.random.fold_in(splits[5], part), 71), part),
    }


def apply_ham(vector, blocks_used, global_rows, global_cols):
    rounded = vector.astype(jnp.bfloat16).astype(jnp.float32)
    forward = jnp.einsum('bij,bjp->bip', blocks_used, rounded[global_cols])
    backward = jnp.einsum('bji,bjp->bip', blocks_used, rounded[global_rows])
    totals = jnp.zeros_like(vector).at[global_rows].add(forward)
    return totals.at[global_cols].add(backward)


def reference(probes, blocks, block_rows, block_cols, counts):
    slots = jnp.arange(DOMAINS * BLK_DEV, dtype=jnp.int32)
    domain = slots // BLK_DEV
    local_slot = slots - domain * BLK_DEV
    used = local_slot < counts[domain]
    blocks_used = jnp.where(used[:, None, None], blocks.astype(jnp.float32), jnp.float32(0.0))
    global_rows = (domain * ATOMS_DEV + block_rows).astype(jnp.int32)
    following = (domain + 1) % DOMAINS
    global_cols = jnp.where(block_cols < ATOMS_DEV, domain * ATOMS_DEV + block_cols,
                            following * ATOMS_DEV + block_cols - ATOMS_DEV).astype(jnp.int32)
    scale = jnp.float32(1.0 / (ATOMS * ORB))
    last_parts = []
    moment_parts = []
    width = 32
    for first in range(0, PROBES, width):
        start_vector = probes[:, :, first:first + width]
        rows = [jnp.sum(start_vector * start_vector, axis=(0, 1)) * scale]
        previous = start_vector
        current = apply_ham(start_vector, blocks_used, global_rows, global_cols)
        rows.append(jnp.sum(start_vector * current, axis=(0, 1)) * scale)
        for step in range(1, STEPS):
            following_vec = 2.0 * apply_ham(current, blocks_used, global_rows, global_cols) - previous
            previous = current
            current = following_vec
            rows.append(jnp.sum(start_vector * current, axis=(0, 1)) * scale)
        last_parts.append(current)
        moment_parts.append(jnp.stack(rows, axis=0))
    return jnp.concatenate(last_parts, axis=2), jnp.concatenate(moment_parts, axis=1)
```

```python
import functools

import jax
import jax.numpy as jnp
from jax import lax
from jax.experimental import pallas as pl
from jax.experimental.pallas import tpu as pltpu
from jax.sharding import PartitionSpec as P

STEPS = 8
RING = ("dom", "orb")
F32, BF16 = jnp.float32, jnp.bfloat16
VMEM = pl.BlockSpec(memory_space=pltpu.VMEM)
SMEM = pl.BlockSpec(memory_space=pltpu.SMEM)


def call(body, outs, flops, *operands, scratch=(), smem=0, limit=16):
    size = sum(o.size * o.dtype.itemsize for o in operands)
    return pl.pallas_call(
        body,
        out_shape=tuple(jax.ShapeDtypeStruct(s, t) for s, t in outs),
        in_specs=[SMEM] * smem + [VMEM] * (len(operands) - smem),
        out_specs=(VMEM,) * len(outs),
        scratch_shapes=scratch,
        compiler_params=pltpu.CompilerParams(vmem_limit_bytes=limit << 20),
        cost_estimate=pl.CostEstimate(flops=flops, bytes_accessed=size, transcendentals=0),
    )(*operands)


def build_body(atoms, orbits, halo, counts, rows, cols, blocks, own_ref, cross_ref, crosst_ref, own_f32, cross_f32):
    chunk = 4 * atoms
    slots = blocks.shape[1]
    slot = lax.broadcasted_iota(jnp.int32, (1, slots), 1)
    pair = jnp.where(slot < counts[0], cols[...] * atoms + rows[...], -1)
    row_id = lax.broadcasted_iota(jnp.int32, (chunk, slots), 0)
    lane = lax.broadcasted_iota(jnp.int32, (orbits, 2 * atoms), 1)

    def place(first, total, target):
        def one(q, _):
            col = first + 4 * q
            onehot = jnp.where(row_id + col * atoms == pair, 1.0, 0.0).astype(BF16)
            tile = lax.dot_general(blocks[...], onehot, (((1,), (1,)), ((), ())), preferred_element_type=F32)
            for two in range(2):
                for i in range(0, orbits, 2):
                    lanes = slice(two * 2 * atoms, (two + 1) * 2 * atoms)
                    left = tile[i * orbits : (i + 1) * orbits, lanes]
                    right = tile[(i + 1) * orbits : (i + 2) * orbits, lanes]
                    low = jnp.where(lane < atoms, left, pltpu.roll(right, atoms, 1))
                    high = jnp.where(lane < atoms, pltpu.roll(left, atoms, 1), right)
                    target[i // 2, pl.ds(4 * q + 2 * two, orbits, stride=total), :] = low
                    target[i // 2, pl.ds(4 * q + 2 * two + 1, orbits, stride=total), :] = high
            return 0

        lax.fori_loop(0, total // 4, one, 0)

    place(0, atoms, own_f32)
    place(atoms, halo, cross_f32)

    size = atoms * orbits
    step = 256
    eye = (
        lax.broadcasted_iota(jnp.int32, (step, step), 0) == lax.broadcasted_iota(jnp.int32, (step, step), 1)
    ).astype(BF16)
    nt = (((1,), (1,)), ((), ()))
    lanes = 2 * atoms
    pieces = size // lanes
    for p in range(pieces):
        crosst_ref[:, p * lanes : (p + 1) * lanes] = cross_f32[p].astype(BF16)
    for t in range(0, size, step):
        part = jnp.concatenate([own_f32[t // lanes + n] for n in range(step // lanes)], axis=1)
        high = part.astype(BF16)
        low = (part - high.astype(F32)).astype(BF16)
        turned = lax.dot_general(eye, high, nt, preferred_element_type=F32)
        turned = turned + lax.dot_general(eye, low, nt, preferred_element_type=F32)
        for p in range(pieces):
            at = slice(p * lanes, (p + 1) * lanes)
            own_ref[t : t + step, at] = (own_f32[p, t : t + step, :] + turned[:, at]).astype(BF16)
        cross_ref[t : t + step, :] = lax.dot_general(
            eye, crosst_ref[:, t : t + step], nt, preferred_element_type=F32
        ).astype(BF16)


def load_body(atoms, orbits, turn, probes, v_ref, w_ref):
    for o in range(orbits):
        v = probes[pl.ds(o, atoms, stride=orbits), :] if turn else probes[o * atoms : (o + 1) * atoms, :]
        v_ref[o * atoms : (o + 1) * atoms, :] = v
        w_ref[o * atoms : (o + 1) * atoms, :] = v.astype(BF16)


def put_sends(atoms, orbits, halo, even, w, products, out_x, out_i):
    for o in range(orbits):
        edge = w[o * atoms : o * atoms + halo, :]
        product = products[o * halo : (o + 1) * halo, :]
        out_x[o * halo : (o + 1) * halo, :] = jnp.where(even, edge, product)
        out_i[o * halo : (o + 1) * halo, :] = jnp.where(even, product, edge)


def first_body(atoms, orbits, halo, parity, w_ref, crosst, out_x, out_i):
    products = jnp.dot(crosst[...], w_ref[...], preferred_element_type=F32).astype(BF16)
    put_sends(atoms, orbits, halo, parity[0] == 0, w_ref, products, out_x, out_i)


def own_body(own, w, v0, v, local_ref, moment_ref):
    local_ref[...] = jnp.dot(own[...], w[...], preferred_element_type=F32)
    moment_ref[...] = jnp.sum(v0[...] * v[...], axis=0, keepdims=True)


def next_vector(atoms, orbits, halo, first, even, got_x, got_i, local, previous, cross, write):
    edge = jnp.where(even, got_i[...], got_x[...])
    total = local[...] + jnp.dot(cross[...], edge, preferred_element_type=F32)
    for o in range(orbits):
        part = total[o * atoms : (o + 1) * atoms, :]
        back = jnp.where(even, got_x[o * halo : (o + 1) * halo, :], got_i[o * halo : (o + 1) * halo, :])
        for at, piece in ((0, part[:halo] + back.astype(F32)), (halo, part[halo:])):
            rows = slice(o * atoms + at, o * atoms + at + piece.shape[0])
            write(o, at, piece if first else 2.0 * piece - previous[rows, :])


def step_body(
    atoms, orbits, halo, first, parity, got_x, got_i, local, previous, cross, crosst, v_ref, w_ref, out_x, out_i
):
    even = parity[0] == 0

    def write(o, at, piece):
        rows = slice(o * atoms + at, o * atoms + at + piece.shape[0])
        v_ref[rows, :] = piece
        w_ref[rows, :] = piece.astype(BF16)

    next_vector(atoms, orbits, halo, first, even, got_x, got_i, local, previous, cross, write)
    products = jnp.dot(crosst[...], w_ref[...], preferred_element_type=F32).astype(BF16)
    put_sends(atoms, orbits, halo, even, w_ref, products, out_x, out_i)


def last_body(atoms, orbits, halo, turn, parity, got_x, got_i, local, previous, cross, v0, out_ref, moment_ref):
    sums = []

    def write(o, at, piece):
        rows = slice(o * atoms + at, o * atoms + at + piece.shape[0])
        out_ref[pl.ds(at * orbits + o, piece.shape[0], stride=orbits) if turn else rows, :] = piece
        sums.append(jnp.sum(v0[rows, :] * piece, axis=0, keepdims=True))

    next_vector(atoms, orbits, halo, False, parity[0] == 0, got_x, got_i, local, previous, cross, write)
    moment_ref[...] = functools.reduce(jnp.add, sums)


def per_device(probes, blocks, block_rows, block_cols, counts):
    atoms, orbits, width = probes.shape
    halo = atoms // 2
    size, edge_size = atoms * orbits, halo * orbits
    slots = blocks.shape[0]
    dims = (atoms, orbits, halo)
    turn = width == 128
    ring = lax.axis_size(RING)
    scale = jnp.float32(1.0 / (size * ring))
    parity = lax.axis_index("orb").astype(jnp.int32).reshape(1)
    between = [(i, (i + 1) % ring) for i in range(1, ring, 2)]
    between = between + [(b, a) for a, b in between]
    inside = [(0, 1), (1, 0)]

    def exchange(send_x, send_i):
        return lax.ppermute(send_x, RING, between), lax.ppermute(send_i, "orb", inside)

    flat = blocks.transpose(1, 2, 0).reshape(orbits * orbits, slots)
    own, cross, crosst = call(
        functools.partial(build_body, *dims),
        (((size, size), BF16), ((size, edge_size), BF16), ((edge_size, size), BF16)),
        2 * orbits * orbits * slots * atoms * (atoms + halo),
        counts,
        block_rows.reshape(1, slots),
        block_cols.reshape(1, slots),
        flat,
        scratch=[
            pltpu.VMEM((orbits // 2, size, 2 * atoms), F32),
            pltpu.VMEM((orbits // 2, edge_size, 2 * atoms), F32),
        ],
        smem=1,
        limit=32,
    )
    v0, w = call(
        functools.partial(load_body, atoms, orbits, turn),
        (((size, width), F32), ((size, width), BF16)),
        0,
        (probes if turn else probes.transpose(1, 0, 2)).reshape(size, width),
    )
    sends = (((edge_size, width), BF16),) * 2
    cross_flops = 2 * size * edge_size * width
    send_x, send_i = call(functools.partial(first_body, *dims), sends, cross_flops, parity, w, crosst, smem=1)
    previous, v = v0, v0
    moments = []
    for k in range(STEPS):
        got_x, got_i = exchange(send_x, send_i)
        local, moment = call(
            own_body, (((size, width), F32), ((1, width), F32)), 2 * size * size * width, own, w, v0, v
        )
        moments.append(moment)
        if k < STEPS - 1:
            following, w, send_x, send_i = call(
                functools.partial(step_body, *dims, k == 0),
                (((size, width), F32), ((size, width), BF16)) + sends,
                2 * cross_flops,
                parity, got_x, got_i, local, previous, cross, crosst,
                smem=1,
            )
            previous, v = v, following
        else:
            last, moment = call(
                functools.partial(last_body, *dims, turn),
                (((size, width), F32), ((1, width), F32)),
                cross_flops,
                parity, got_x, got_i, local, previous, cross, v0,
                smem=1,
            )
            moments.append(moment)
    table = lax.psum(jnp.concatenate(moments, axis=0) * scale, RING)
    last = last.reshape(atoms, orbits, width) if turn else last.reshape(orbits, atoms, width).transpose(1, 0, 2)
    return last, table


def solution(mesh):
    in_specs = (
        P(("groups", "dom", "orb"), None, "probe"),
        P(("groups", "dom", "orb"), None, None),
        P(("groups", "dom", "orb")),
        P(("groups", "dom", "orb")),
        P(("groups", "dom", "orb")),
    )
    out_specs = (P(("groups", "dom", "orb"), None, "probe"), P("groups", "probe"))
    return jax.shard_map(
        per_device, mesh=mesh, in_specs=in_specs, out_specs=out_specs, check_vma=False
    )
```

```python
import functools

import jax
import jax.numpy as jnp
from jax import lax
from jax.experimental import pallas as pl
from jax.experimental.pallas import tpu as pltpu
from jax.sharding import PartitionSpec as P

STEPS = 8
RING = ("dom", "orb")
F32, BF16 = jnp.float32, jnp.bfloat16
VMEM = pl.BlockSpec(memory_space=pltpu.VMEM)
SMEM = pl.BlockSpec(memory_space=pltpu.SMEM)
NT = (((1,), (1,)), ((), ()))
UNROLL = 8
PAD = 8
HALF = STEPS // 2
DOTS = [
    [(0, n)] + [(m, n) for m in (n - 1, n) if m > 0 and HALF < m + n] for n in range(HALF + 1)
]


def operands_of(k):
    return sorted({m for pair in DOTS[k] for m in pair})


def call(body, outs, flops, *operands, scratch=(), smem=0, limit=16):
    size = sum(o.size * o.dtype.itemsize for o in operands)
    return pl.pallas_call(
        body,
        out_shape=tuple(jax.ShapeDtypeStruct(s, t) for s, t in outs),
        in_specs=[SMEM] * smem + [VMEM] * (len(operands) - smem),
        out_specs=(VMEM,) * len(outs),
        scratch_shapes=scratch,
        compiler_params=pltpu.CompilerParams(vmem_limit_bytes=limit << 20),
        cost_estimate=pl.CostEstimate(flops=flops, bytes_accessed=size, transcendentals=0),
    )(*operands)


def build_body(atoms, orbits, halo, pair, blocks, own_ref, cross_ref, crosst_ref, own_f32, cross_f32, row_hot):
    slots = blocks.shape[1]
    pair_id = pair[...].reshape(1, slots)
    col_id = lax.div(pair_id, atoms)
    row_id = pair_id - col_id * atoms
    row_hot[...] = jnp.where(lax.broadcasted_iota(jnp.int32, (atoms, slots), 0) == row_id, 1.0, 0.0).astype(BF16)
    lanes = 2 * atoms
    lane = lax.broadcasted_iota(jnp.int32, (orbits, lanes), 1)

    def place(first, total, target):
        def one(q, _):
            hot = []
            for n in range(4):
                here = jnp.where(col_id == first + 4 * q + n, 1.0, 0.0).astype(BF16)
                hot.append(row_hot[...] * here)
            hot = jnp.concatenate(hot, axis=0)
            tile = lax.dot_general(blocks[...], hot, NT, preferred_element_type=F32)
            for two in range(2):
                for i in range(0, orbits, 2):
                    at = slice(two * lanes, (two + 1) * lanes)
                    left = tile[i * orbits : (i + 1) * orbits, at]
                    right = tile[(i + 1) * orbits : (i + 2) * orbits, at]
                    low = jnp.where(lane < atoms, left, pltpu.roll(right, atoms, 1))
                    high = jnp.where(lane < atoms, pltpu.roll(left, atoms, 1), right)
                    col = 4 * q + 2 * two
                    target[i // 2, pl.ds(col, orbits, stride=total + PAD), :] = low
                    target[i // 2, pl.ds(col + 1, orbits, stride=total + PAD), :] = high
            return 0

        lax.fori_loop(0, total // 4, one, 0, unroll=UNROLL)

    place(0, atoms, own_f32)
    place(atoms, halo, cross_f32)

    def rows(source, piece, total):
        apart = [source[piece, j * (total + PAD) : j * (total + PAD) + total, :] for j in range(orbits)]
        return jnp.concatenate(apart, axis=0)

    for p in range(orbits // 2):
        at = slice(p * lanes, (p + 1) * lanes)
        mine = rows(cross_f32, p, halo)
        crosst_ref[:, at] = mine.astype(BF16)
        cross_ref[at, :] = mine.T.astype(BF16)
        turned = rows(own_f32, p, atoms).T
        for n in range(orbits // 2):
            here = slice(n * lanes, (n + 1) * lanes)
            starts = [(2 * p + m) * (atoms + PAD) for m in range(2)]
            other = jnp.concatenate([own_f32[n, start : start + atoms, :] for start in starts], axis=0)
            own_ref[at, here] = (other + turned[:, here]).astype(BF16)


def put_sends(atoms, orbits, halo, even, w, products, out_x, out_i):
    for o in range(orbits):
        edge = w[o * atoms : o * atoms + halo, :]
        product = products[o * halo : (o + 1) * halo, :]
        out_x[o * halo : (o + 1) * halo, :] = jnp.where(even, edge, product)
        out_i[o * halo : (o + 1) * halo, :] = jnp.where(even, product, edge)


def first_body(atoms, orbits, halo, turn, parity, probes, crosst, v_ref, w_ref, out_x, out_i):
    for o in range(orbits):
        rows = slice(o * atoms, (o + 1) * atoms)
        v = probes[pl.ds(o, atoms, stride=orbits), :] if turn else probes[rows, :]
        v_ref[rows, :] = v
        w_ref[rows, :] = v.astype(BF16)
    products = jnp.dot(crosst[...], w_ref[...], preferred_element_type=F32).astype(BF16)
    put_sends(atoms, orbits, halo, parity[0] == 0, w_ref, products, out_x, out_i)


def own_body(k, scale, own, w, *refs):
    local_ref, table_ref = refs[-2:]
    local_ref[...] = jnp.dot(own[...], w[...], preferred_element_type=F32)
    if k > HALF:
        table_ref[...] = refs[0][...] + refs[1][...]
        return
    vectors = dict(zip(operands_of(k), refs))
    made = [jnp.sum(vectors[m][...] * vectors[n][...], axis=0, keepdims=True) for m, n in DOTS[k]]
    if k < HALF:
        table_ref[...] = jnp.concatenate(made, axis=0)
        return
    dots = dict(zip(DOTS[k], made))
    for table, pairs in zip(refs[len(vectors) : -2], DOTS):
        dots.update({pair: table[n : n + 1, :] for n, pair in enumerate(pairs)})
    rows = []
    for n in range(STEPS + 1):
        if n <= HALF:
            rows.append(dots[0, n])
        else:
            rows.append(2.0 * dots[n // 2, n - n // 2] - dots[0, n % 2])
    table_ref[...] = jnp.concatenate(rows, axis=0) * scale


def next_vector(atoms, orbits, halo, first, even, got_x, got_i, local, previous, cross, write):
    edge = jnp.where(even, got_i[...], got_x[...])
    total = local[...] + jnp.dot(cross[...], edge, preferred_element_type=F32)
    for o in range(orbits):
        part = total[o * atoms : (o + 1) * atoms, :]
        back = jnp.where(even, got_x[o * halo : (o + 1) * halo, :], got_i[o * halo : (o + 1) * halo, :])
        for at, piece in ((0, part[:halo] + back.astype(F32)), (halo, part[halo:])):
            rows = slice(o * atoms + at, o * atoms + at + piece.shape[0])
            write(o, at, piece if first else 2.0 * piece - previous[rows, :])


def step_body(
    atoms, orbits, halo, first, parity, got_x, got_i, local, previous, cross, crosst, v_ref, w_ref, out_x, out_i
):
    even = parity[0] == 0

    def write(o, at, piece):
        rows = slice(o * atoms + at, o * atoms + at + piece.shape[0])
        v_ref[rows, :] = piece
        w_ref[rows, :] = piece.astype(BF16)

    next_vector(atoms, orbits, halo, first, even, got_x, got_i, local, previous, cross, write)
    products = jnp.dot(crosst[...], w_ref[...], preferred_element_type=F32).astype(BF16)
    put_sends(atoms, orbits, halo, even, w_ref, products, out_x, out_i)


def last_body(atoms, orbits, halo, turn, parity, got_x, got_i, local, previous, cross, out_ref):
    def write(o, at, piece):
        rows = slice(o * atoms + at, o * atoms + at + piece.shape[0])
        out_ref[pl.ds(at * orbits + o, piece.shape[0], stride=orbits) if turn else rows, :] = piece

    next_vector(atoms, orbits, halo, False, parity[0] == 0, got_x, got_i, local, previous, cross, write)


def sum_rounds():
    doms = lax.axis_size("dom")
    swap = lambda axis, bit: lambda x: lax.ppermute(x, axis, [(i, i ^ bit) for i in range(lax.axis_size(axis))])
    if doms & (doms - 1):
        return [lambda x: lax.psum(x, RING) - x]
    return [swap("orb", 1)] + [swap("dom", 1 << n) for n in range(doms.bit_length() - 1)]


def per_device(probes, blocks, block_rows, block_cols, counts):
    atoms, orbits, width = probes.shape
    halo = atoms // 2
    size, edge_size = atoms * orbits, halo * orbits
    slots = blocks.shape[0]
    dims = (atoms, orbits, halo)
    turn = width == 128
    ring = lax.axis_size(RING)
    scale = 1.0 / (size * ring)
    parity = lax.axis_index("orb").astype(jnp.int32).reshape(1)
    between = [(i, (i + 1) % ring) for i in range(1, ring, 2)]
    between = between + [(b, a) for a, b in between]
    inside = [(0, 1), (1, 0)]

    def exchange(send_x, send_i):
        return lax.ppermute(send_x, RING, between), lax.ppermute(send_i, "orb", inside)

    slot = jnp.arange(slots, dtype=jnp.int32)
    pair = jnp.where(slot < counts[0], block_cols * atoms + block_rows, -atoms)
    own, cross, crosst = call(
        functools.partial(build_body, *dims),
        (((size, size), BF16), ((size, edge_size), BF16), ((edge_size, size), BF16)),
        2 * orbits * orbits * slots * atoms * (atoms + halo),
        pair,
        blocks.transpose(1, 2, 0).reshape(orbits * orbits, slots),
        scratch=[
            pltpu.VMEM((orbits // 2, orbits * (atoms + PAD), 2 * atoms), F32),
            pltpu.VMEM((orbits // 2, orbits * (halo + PAD), 2 * atoms), F32),
            pltpu.VMEM((atoms, slots), BF16),
        ],
        limit=32,
    )
    vector = (((size, width), F32), ((size, width), BF16))
    sends = (((edge_size, width), BF16),) * 2
    cross_flops = 2 * size * edge_size * width
    v, w, send_x, send_i = call(
        functools.partial(first_body, *dims, turn),
        vector + sends,
        cross_flops,
        parity,
        (probes if turn else probes.transpose(1, 0, 2)).reshape(size, width),
        crosst,
        smem=1,
    )
    vectors, tables, rounds = [v], [], sum_rounds()
    table = None
    for k in range(STEPS):
        got_x, got_i = exchange(send_x, send_i)
        if k <= HALF:
            extra = [vectors[m] for m in operands_of(k)] + (tables if k == HALF else [])
        else:
            extra = [table, rounds.pop(0)(table) if rounds else jnp.zeros_like(table)]
        height = len(DOTS[k]) if k < HALF else STEPS + 1
        local, table = call(
            functools.partial(own_body, k, scale),
            (((size, width), F32), ((height, width), F32)),
            2 * size * size * width,
            own, w, *extra,
        )
        tables.append(table)
        operands = (parity, got_x, got_i, local, vectors[max(k - 1, 0)], cross)
        if k < STEPS - 1:
            v, w, send_x, send_i = call(
                functools.partial(step_body, *dims, k == 0), vector + sends, 2 * cross_flops, *operands, crosst, smem=1
            )
            vectors.append(v)
        else:
            (last,) = call(functools.partial(last_body, *dims, turn), vector[:1], cross_flops, *operands, smem=1)
    for one in rounds:
        table = table + one(table)
    last = last.reshape(atoms, orbits, width) if turn else last.reshape(orbits, atoms, width).transpose(1, 0, 2)
    return last, table


def solution(mesh):
    in_specs = (
        P(("groups", "dom", "orb"), None, "probe"),
        P(("groups", "dom", "orb"), None, None),
        P(("groups", "dom", "orb")),
        P(("groups", "dom", "orb")),
        P(("groups", "dom", "orb")),
    )
    out_specs = (P(("groups", "dom", "orb"), None, "probe"), P("groups", "probe"))
    return jax.shard_map(
        per_device, mesh=mesh, in_specs=in_specs, out_specs=out_specs, check_vma=False
    )
```

```python
import functools

import jax
import jax.numpy as jnp
from jax import lax
from jax.experimental import pallas as pl
from jax.experimental.pallas import tpu as pltpu
from jax.sharding import PartitionSpec as P

STEPS = 8
HALF = STEPS // 2
RING = ("dom", "orb")
F32, BF16 = jnp.float32, jnp.bfloat16
VMEM = pl.BlockSpec(memory_space=pltpu.VMEM)
SMEM = pl.BlockSpec(memory_space=pltpu.SMEM)
NT = (((1,), (1,)), ((), ()))
UNROLL = 8
PAD = 8
ROWS = 16
TAIL = 3 * ROWS
LONGER = ROWS
DOTS = [[(0, n)] + [(m, n) for m in (n - 1, n) if m > 0 and HALF < m + n] for n in range(HALF + 1)]


def operands_of(n):
    return sorted({m for pair in DOTS[n] for m in pair})


def call(body, outs, *operands, flops=0, scratch=(), smem=0, limit=16):
    size = sum(o.size * o.dtype.itemsize for o in operands)
    return pl.pallas_call(
        body,
        out_shape=tuple(jax.ShapeDtypeStruct(s, t) for s, t in outs),
        in_specs=[SMEM] * smem + [VMEM] * (len(operands) - smem),
        out_specs=(VMEM,) * len(outs),
        scratch_shapes=scratch,
        compiler_params=pltpu.CompilerParams(vmem_limit_bytes=limit << 20),
        cost_estimate=pl.CostEstimate(flops=flops, bytes_accessed=size, transcendentals=0) if flops else None,
    )(*operands)


def place(atoms, orbits, first, total, pair, blocks, target, row_hot):
    slots = blocks.shape[1]
    pair_id = pair[...].reshape(1, slots)
    col_id = lax.div(pair_id, atoms)
    row_id = pair_id - col_id * atoms
    row_hot[...] = jnp.where(lax.broadcasted_iota(jnp.int32, (atoms, slots), 0) == row_id, 1.0, 0.0).astype(BF16)
    lanes = 2 * atoms
    lane = lax.broadcasted_iota(jnp.int32, (orbits, lanes), 1)

    def one(q, _):
        hot = []
        for n in range(4):
            here = jnp.where(col_id == first + 4 * q + n, 1.0, 0.0).astype(BF16)
            hot.append(row_hot[...] * here)
        hot = jnp.concatenate(hot, axis=0)
        tile = lax.dot_general(blocks[...], hot, NT, preferred_element_type=F32)
        for two in range(2):
            for i in range(0, orbits, 2):
                at = slice(two * lanes, (two + 1) * lanes)
                left = tile[i * orbits : (i + 1) * orbits, at]
                right = tile[(i + 1) * orbits : (i + 2) * orbits, at]
                low = jnp.where(lane < atoms, left, pltpu.roll(right, atoms, 1))
                high = jnp.where(lane < atoms, pltpu.roll(left, atoms, 1), right)
                col = 4 * q + 2 * two
                target[i // 2, pl.ds(col, orbits, stride=total + PAD), :] = low
                target[i // 2, pl.ds(col + 1, orbits, stride=total + PAD), :] = high
        return 0

    lax.fori_loop(0, total // 4, one, 0, unroll=UNROLL)


def gather_rows(source, piece, total, orbitals):
    starts = [j * (total + PAD) for j in orbitals]
    return jnp.concatenate([source[piece, start : start + total, :] for start in starts], axis=0)


def cross_body(atoms, orbits, halo, pair, blocks, crosst_ref, cross_f32, row_hot):
    place(atoms, orbits, atoms, halo, pair, blocks, cross_f32, row_hot)
    lanes = 2 * atoms
    for p in range(orbits // 2):
        at = slice(p * lanes, (p + 1) * lanes)
        crosst_ref[:, at] = gather_rows(cross_f32, p, halo, range(orbits)).astype(BF16)


def own_body(atoms, orbits, halo, pair, blocks, crosst, _, own_ref, cross_ref, gram_ref, own_f32, row_hot):
    place(atoms, orbits, 0, atoms, pair, blocks, own_f32, row_hot)
    lanes = 2 * atoms
    for p in range(orbits // 2):
        at = slice(p * lanes, (p + 1) * lanes)
        cross_ref[at, :] = crosst[:, at].astype(F32).T.astype(BF16)
        turned = gather_rows(own_f32, p, atoms, range(orbits)).T
        for n in range(orbits // 2):
            here = slice(n * lanes, (n + 1) * lanes)
            other = gather_rows(own_f32, n, atoms, (2 * p, 2 * p + 1))
            own_ref[at, here] = (other + turned[:, here]).astype(BF16)
    gram_ref[...] = jnp.dot(crosst[...], cross_ref[...], preferred_element_type=F32).astype(BF16)


def put_edge(atoms, halo, w, out):
    for o in range(w.shape[0] // atoms):
        out[o * halo : (o + 1) * halo, :] = w[o * atoms : o * atoms + halo, :]


def blank(out, start):
    out[start:, :] = jnp.zeros((out.shape[0] - start, out.shape[1]), out.dtype)


def times(left, right):
    return jnp.dot(left[...], right[...], preferred_element_type=F32)


def first_body(atoms, orbits, halo, turn, parity, probes, crosst, v_ref, w_ref, out_x, out_i):
    for o in range(orbits):
        rows = slice(o * atoms, (o + 1) * atoms)
        v = probes[pl.ds(o, atoms, stride=orbits), :] if turn else probes[rows, :]
        v_ref[rows, :] = v
        w_ref[rows, :] = v.astype(BF16)

    @pl.when(parity[0] == 0)
    def _():
        put_edge(atoms, halo, w_ref, out_x)
        out_i[...] = times(crosst, w_ref).astype(BF16)

    blank(out_x, orbits * halo)

    @pl.when(parity[0] != 0)
    def _():
        put_edge(atoms, halo, w_ref, out_i)
        out_x[: orbits * halo, :] = times(crosst, w_ref).astype(BF16)


def dots_of(n, refs):
    vectors = dict(zip(operands_of(n), refs))
    return [jnp.sum(vectors[a][...] * vectors[b][...], axis=0, keepdims=True) for a, b in DOTS[n]]


def local_body(k, own, w, *refs):
    refs[-1 if k >= HALF else -2][...] = times(own, w)
    if k < HALF:
        refs[-1][...] = jnp.concatenate(dots_of(k, refs), axis=0)


def table_of(scale, made, tables):
    dots = dict(zip(DOTS[HALF], made))
    for table, pairs in zip(tables, DOTS):
        dots.update({pair: table[n : n + 1, :] for n, pair in enumerate(pairs)})
    rows = [dots[0, n] for n in range(HALF + 1)]
    for n in range(HALF + 1, STEPS + 1):
        rows.append(2.0 * dots[n // 2, n - n // 2] - dots[0, n % 2])
    rows.append(jnp.zeros((ROWS - STEPS - 1, rows[0].shape[1]), F32))
    return jnp.concatenate(rows, axis=0) * scale


def put_table(table, out, start):
    for n in range(3):
        piece = table.astype(BF16)
        out[start + n * ROWS : start + (n + 1) * ROWS, :] = piece
        table = table - piece.astype(F32)


def get_table(got, start):
    pieces = [got[start + n * ROWS : start + (n + 1) * ROWS, :].astype(F32) for n in range(3)]
    return pieces[0] + (pieces[1] + pieces[2])


def before_body(atoms, orbits, halo, k, parity, got_i, local, previous, cross, crosst, base_ref, pre_ref=None):
    edge_size = orbits * halo
    grown = lambda total, rows: total if k == 0 else 2.0 * total - previous[rows, :]

    @pl.when(parity[0] == 0)
    def _():
        total = local[...] + times(cross, got_i[:edge_size, :])
        base_ref[...] = grown(total, slice(None))
        if pre_ref is not None:
            put_edge(atoms, halo, base_ref, pre_ref)

    @pl.when(parity[0] != 0)
    def _():
        for o in range(orbits):
            near = slice(o * atoms, o * atoms + halo)
            far = slice(o * atoms + halo, (o + 1) * atoms)
            back = got_i[o * halo : (o + 1) * halo, :].astype(F32)
            base_ref[near, :] = grown(local[near, :] + back, near)
            base_ref[far, :] = grown(local[far, :], far)
        if pre_ref is not None:
            pre_ref[...] = times(crosst, base_ref[...].astype(BF16))


def send_body(k, tail, parity, got_x, pre, gram, *refs):
    out = refs[-1]
    edge_size = pre.shape[0]
    factor = 1.0 if k == 0 else 2.0

    @pl.when(parity[0] == 0)
    def _():
        out[:edge_size, :] = (pre[...] + factor * got_x[:edge_size, :].astype(F32)).astype(BF16)

    @pl.when(parity[0] != 0)
    def _():
        out[:edge_size, :] = (pre[...] + factor * times(gram, got_x[:edge_size, :])).astype(BF16)

    if tail == "sum":
        table, got = refs[:-1]
        put_table(table[...] + get_table(got, edge_size), out, edge_size)
        blank(out, edge_size + TAIL)
    elif tail == "pass":
        out[edge_size : edge_size + TAIL, :] = refs[0][edge_size : edge_size + TAIL, :]
        blank(out, edge_size + TAIL)
    else:
        blank(out, edge_size)


def finish(atoms, orbits, halo, k, parity, got_x, base, cross, write):
    factor = 1.0 if k == 0 else 2.0

    @pl.when(parity[0] == 0)
    def _():
        for o in range(orbits):
            near = slice(o * atoms, o * atoms + halo)
            back = got_x[o * halo : (o + 1) * halo, :].astype(F32)
            write(o, 0, base[near, :] + factor * back)
            write(o, halo, base[o * atoms + halo : (o + 1) * atoms, :])

    @pl.when(parity[0] != 0)
    def _():
        total = base[...] + factor * times(cross, got_x[: orbits * halo, :])
        for o in range(orbits):
            write(o, 0, total[o * atoms : (o + 1) * atoms, :])


def next_body(atoms, orbits, halo, k, tail, scale, ride, parity, got_x, base, cross, crosst, _, *refs):
    keep = k < STEPS - 2
    outs = refs[len(refs) - 2 - keep - (tail == "start") :]
    (v_ref, w_ref, out) = outs[:3] if keep else (None, *outs)
    edge_size = orbits * halo

    def write(o, at, piece):
        rows = slice(o * atoms + at, o * atoms + at + piece.shape[0])
        if keep:
            v_ref[rows, :] = piece
        w_ref[rows, :] = piece.astype(BF16)

    finish(atoms, orbits, halo, k, parity, got_x, base, cross, write)

    @pl.when(parity[0] == 0)
    def _():
        out[:edge_size, :] = times(crosst, w_ref).astype(BF16)

    @pl.when(parity[0] != 0)
    def _():
        put_edge(atoms, halo, w_ref, out)

    if tail == "start":
        others = operands_of(HALF)[:-1]
        made = dots_of(HALF, refs[: len(others)] + (v_ref,))
        table = table_of(scale, made, refs[len(others) : len(others) + HALF])
        outs[3][...] = table
        if ride:
            put_table(table, out, edge_size)
    elif tail == "pass":
        out[edge_size:, :] = got_x[edge_size : edge_size + TAIL, :]


def last_body(atoms, orbits, halo, k, turn, parity, got_x, base, cross, table, *refs):
    out, moments = refs[-2:]
    edge_size = orbits * halo

    def write(o, at, piece):
        rows = slice(o * atoms + at, o * atoms + at + piece.shape[0])
        out[pl.ds(at * orbits + o, piece.shape[0], stride=orbits) if turn else rows, :] = piece

    finish(atoms, orbits, halo, k, parity, got_x, base, cross, write)
    total = table[...]
    for got in refs[:-2]:
        total = total + get_table(got, edge_size)
    moments[...] = total[: STEPS + 1, :]


def per_device(probes, blocks, block_rows, block_cols, counts):
    atoms, orbits, width = probes.shape
    halo = atoms // 2
    size, edge_size = atoms * orbits, halo * orbits
    slots = blocks.shape[0]
    dims = (atoms, orbits, halo)
    turn = width == 128
    ring = lax.axis_size(RING)
    ride = ring == STEPS
    scale = 1.0 / (size * ring)
    parity = lax.axis_index("orb").astype(jnp.int32).reshape(1)
    between = [(i, (i + 1) % ring) for i in range(1, ring, 2)]
    between = between + [(b, a) for a, b in between]
    across = lambda x: lax.ppermute(x, RING, between)
    inside = lambda x: lax.ppermute(x, "orb", [(0, 1), (1, 0)])

    slot = jnp.arange(slots, dtype=jnp.int32)
    pair = jnp.where(slot < counts[0], block_cols * atoms + block_rows, -atoms)
    flat = blocks.transpose(1, 2, 0).reshape(orbits * orbits, slots)
    row_hot = pltpu.VMEM((atoms, slots), BF16)
    (crosst,) = call(
        functools.partial(cross_body, *dims),
        (((edge_size, size), BF16),),
        pair, flat,
        flops=2 * orbits * orbits * slots * atoms * halo,
        scratch=[pltpu.VMEM((orbits // 2, orbits * (halo + PAD), 2 * atoms), F32), row_hot],
        limit=24,
    )
    whole, rounded, message = ((size, width), F32), ((size, width), BF16), ((edge_size, width), BF16)
    longer = ((edge_size + TAIL, width), BF16)
    far_rows = [edge_size + LONGER + (TAIL if ride and k >= HALF else 0) for k in range(STEPS)]
    v, w, send_x, send_i = call(
        functools.partial(first_body, *dims, turn),
        (whole, rounded, ((far_rows[0], width), BF16), message),
        parity,
        (probes if turn else probes.transpose(1, 0, 2)).reshape(size, width),
        crosst,
        smem=1,
    )
    vectors, tables, got = [v], [], []
    for k in range(STEPS):
        got_x = across(send_x)
        if k > 0:
            tail = {HALF: "start", HALF + 2: "pass"}.get(k) if ride or k == HALF else None
            extra, outs = (), (whole, rounded, longer if tail and ride else message)[k == STEPS - 1 :]
            if k == HALF:
                extra, outs = (*(vectors[m] for m in operands_of(HALF)[:-1]), *tables), outs + (((ROWS, width), F32),)
            made = call(
                functools.partial(next_body, *dims, k - 1, tail, scale, ride),
                outs, parity, arrived, base, cross, crosst, send_x, *extra, smem=1,
            )
            if k < STEPS - 1:
                vectors.append(made[0])
            w, send_i = made[k < STEPS - 1 :][:2]
            if k == HALF:
                table = made[3]
        got_i = inside(send_i)
        if k == 0:
            own, cross, gram = call(
                functools.partial(own_body, *dims),
                (((size, size), BF16), ((size, edge_size), BF16), ((edge_size, edge_size), BF16)),
                pair, flat, crosst, send_i,
                scratch=[pltpu.VMEM((orbits // 2, orbits * (atoms + PAD), 2 * atoms), F32), row_hot],
                limit=24,
            )
        dots = ()
        if k < HALF:
            dots = (((len(DOTS[k]), width), F32),)
        made = call(
            functools.partial(local_body, k),
            (whole,) + dots,
            own, w, *((vectors[m] for m in operands_of(k)) if k < HALF else ()),
        )
        local, tables = made[0], tables + list(made[1:])
        base, *pre = call(
            functools.partial(before_body, *dims, k),
            (whole, ((edge_size, width), F32))[: 2 - (k == STEPS - 1)],
            parity, got_i, local, vectors[max(k - 1, 0)], cross, crosst, smem=1,
        )
        arrived = got_x
        if k < STEPS - 1:
            tail = {HALF: "sum", HALF + 2: "pass"}.get(k) if ride else None
            extra = {"sum": (table, got_i), "pass": (got_i,)}[tail] if tail else ()
            (send_x,) = call(
                functools.partial(send_body, k, tail),
                (((far_rows[k + 1], width), BF16),),
                parity, got_x, *pre, gram, *extra, smem=1,
            )
        if ride and k >= HALF:
            got.append(got_i if k % 2 == 0 else got_x)
    last, moments = call(
        functools.partial(last_body, *dims, STEPS - 1, turn),
        (whole, ((STEPS + 1, width), F32)),
        parity, got_x, base, cross, table, *got, smem=1,
    )
    last = last.reshape(atoms, orbits, width) if turn else last.reshape(orbits, atoms, width).transpose(1, 0, 2)
    return last, moments if ride else lax.psum(moments, RING)


def solution(mesh):
    in_specs = (
        P(("groups", "dom", "orb"), None, "probe"),
        P(("groups", "dom", "orb"), None, None),
        P(("groups", "dom", "orb")),
        P(("groups", "dom", "orb")),
        P(("groups", "dom", "orb")),
    )
    out_specs = (P(("groups", "dom", "orb"), None, "probe"), P("groups", "probe"))
    return jax.shard_map(
        per_device, mesh=mesh, in_specs=in_specs, out_specs=out_specs, check_vma=False
    )
```

```python
import functools

import jax
import jax.numpy as jnp
from jax import lax
from jax.experimental import pallas as pl
from jax.experimental.pallas import tpu as pltpu
from jax.sharding import PartitionSpec as P

STEPS = 8
HALF = STEPS // 2
RING = ("dom", "orb")
F32, BF16 = jnp.float32, jnp.bfloat16
VMEM = pl.BlockSpec(memory_space=pltpu.VMEM)
SMEM = pl.BlockSpec(memory_space=pltpu.SMEM)
NT = (((1,), (1,)), ((), ()))
PAD = 8
ROWS = 16
TAIL = 3 * ROWS
LONGER = ROWS
DOTS = [[(0, n)] + [(m, n) for m in (n - 1, n) if m > 0 and HALF < m + n] for n in range(HALF + 1)]
DOTS[:2] = [[], DOTS[0] + DOTS[1]]


def operands_of(n):
    return sorted({m for pair in DOTS[n] for m in pair})


def call(body, outs, *operands, flops=0, scratch=(), smem=0, limit=16):
    size = sum(o.size * o.dtype.itemsize for o in operands)
    return pl.pallas_call(
        body,
        out_shape=tuple(jax.ShapeDtypeStruct(s, t) for s, t in outs),
        in_specs=[SMEM] * smem + [VMEM] * (len(operands) - smem),
        out_specs=(VMEM,) * len(outs),
        scratch_shapes=scratch,
        compiler_params=pltpu.CompilerParams(vmem_limit_bytes=limit << 20),
        cost_estimate=pl.CostEstimate(flops=flops, bytes_accessed=size, transcendentals=0) if flops else None,
    )(*operands)


def place(atoms, orbits, first, total, pair, blocks, target, row_hot):
    slots = blocks.shape[1]
    pair_id = pair[...].reshape(1, slots)
    col_id = lax.div(pair_id, atoms)
    row_id = pair_id - col_id * atoms
    row_hot[...] = jnp.where(lax.broadcasted_iota(jnp.int32, (atoms, slots), 0) == row_id, 1.0, 0.0).astype(BF16)
    lanes = 2 * atoms
    lane = lax.broadcasted_iota(jnp.int32, (orbits, lanes), 1)

    def one(q, _):
        hot = []
        for n in range(4):
            here = jnp.where(col_id == first + 4 * q + n, 1.0, 0.0).astype(BF16)
            hot.append(row_hot[...] * here)
        hot = jnp.concatenate(hot, axis=0)
        tile = lax.dot_general(blocks[...], hot, NT, preferred_element_type=F32)
        for two in range(2):
            for i in range(0, orbits, 2):
                at = slice(two * lanes, (two + 1) * lanes)
                left = tile[i * orbits : (i + 1) * orbits, at]
                right = tile[(i + 1) * orbits : (i + 2) * orbits, at]
                low = jnp.where(lane < atoms, left, pltpu.roll(right, atoms, 1))
                high = jnp.where(lane < atoms, pltpu.roll(left, atoms, 1), right)
                col = 4 * q + 2 * two
                target[i // 2, pl.ds(col, orbits, stride=total + PAD), :] = low
                target[i // 2, pl.ds(col + 1, orbits, stride=total + PAD), :] = high
        return 0

    lax.fori_loop(0, total // 4, one, 0, unroll=total // 4)


def gather_rows(source, piece, total, orbitals):
    starts = [j * (total + PAD) for j in orbitals]
    return jnp.concatenate([source[piece, start : start + total, :] for start in starts], axis=0)


def cross_body(atoms, orbits, halo, pair, blocks, crosst_ref, cross_f32, row_hot):
    place(atoms, orbits, atoms, halo, pair, blocks, cross_f32, row_hot)
    lanes = 2 * atoms
    for p in range(orbits // 2):
        at = slice(p * lanes, (p + 1) * lanes)
        crosst_ref[:, at] = gather_rows(cross_f32, p, halo, range(orbits)).astype(BF16)


def own_body(atoms, orbits, halo, pair, blocks, crosst, w, _, own_ref, cross_ref, gram_ref, local_ref, own_f32, row_hot):
    place(atoms, orbits, 0, atoms, pair, blocks, own_f32, row_hot)
    gram_ref[...] = lax.dot_general(crosst[...], crosst[...], NT, preferred_element_type=F32).astype(BF16)
    lanes = 2 * atoms
    for p in range(orbits // 2):
        at = slice(p * lanes, (p + 1) * lanes)
        cross_ref[at, :] = crosst[:, at].astype(F32).T.astype(BF16)
        turned = gather_rows(own_f32, p, atoms, range(orbits)).T
        parts = []
        for n in range(orbits // 2):
            other = gather_rows(own_f32, n, atoms, (2 * p, 2 * p + 1))
            parts.append((other + turned[:, n * lanes : (n + 1) * lanes]).astype(BF16))
        mine = jnp.concatenate(parts, axis=1)
        own_ref[at, :] = mine
        local_ref[at, :] = times(mine, w)


def put_edge(atoms, halo, w, out):
    for o in range(w.shape[0] // atoms):
        out[o * halo : (o + 1) * halo, :] = w[o * atoms : o * atoms + halo, :]


def blank(out, start):
    out[start:, :] = jnp.zeros((out.shape[0] - start, out.shape[1]), out.dtype)


def times(left, right):
    return jnp.dot(left[...], right[...], preferred_element_type=F32)


def first_body(atoms, orbits, halo, turn, parity, probes, crosst, v_ref, w_ref, out_x, out_i):
    for o in range(orbits):
        rows = slice(o * atoms, (o + 1) * atoms)
        v = probes[pl.ds(o, atoms, stride=orbits), :] if turn else probes[rows, :]
        v_ref[rows, :] = v
        w_ref[rows, :] = v.astype(BF16)

    @pl.when(parity[0] == 0)
    def _():
        put_edge(atoms, halo, w_ref, out_x)
        out_i[...] = times(crosst, w_ref).astype(BF16)

    blank(out_x, orbits * halo)

    @pl.when(parity[0] != 0)
    def _():
        put_edge(atoms, halo, w_ref, out_i)
        out_x[: orbits * halo, :] = times(crosst, w_ref).astype(BF16)


def dots_of(n, refs):
    vectors = dict(zip(operands_of(n), refs))
    return [jnp.sum(vectors[a][...] * vectors[b][...], axis=0, keepdims=True) for a, b in DOTS[n]]


def local_body(k, own, w, *refs):
    refs[-1 if k >= HALF else -2][...] = times(own, w)
    if k < HALF:
        refs[-1][...] = jnp.concatenate(dots_of(k, refs), axis=0)


def table_of(scale, made, tables):
    dots = dict(zip(DOTS[HALF], made))
    for table, pairs in zip(tables, DOTS[1:]):
        dots.update({pair: table[n : n + 1, :] for n, pair in enumerate(pairs)})
    rows = [dots[0, n] for n in range(HALF + 1)]
    for n in range(HALF + 1, STEPS + 1):
        rows.append(2.0 * dots[n // 2, n - n // 2] - dots[0, n % 2])
    rows.append(jnp.zeros((ROWS - STEPS - 1, rows[0].shape[1]), F32))
    return jnp.concatenate(rows, axis=0) * scale


def put_table(table, out, start):
    for n in range(3):
        piece = table.astype(BF16)
        out[start + n * ROWS : start + (n + 1) * ROWS, :] = piece
        table = table - piece.astype(F32)


def get_table(got, start):
    pieces = [got[start + n * ROWS : start + (n + 1) * ROWS, :].astype(F32) for n in range(3)]
    return pieces[0] + (pieces[1] + pieces[2])


def before_body(atoms, orbits, halo, k, parity, got_i, local, previous, cross, crosst, base_ref, pre_ref=None):
    edge_size = orbits * halo
    grown = lambda total, rows: total if k == 0 else 2.0 * total - previous[rows, :]

    @pl.when(parity[0] == 0)
    def _():
        total = local[...] + times(cross, got_i[:edge_size, :])
        base_ref[...] = grown(total, slice(None))
        if pre_ref is not None:
            put_edge(atoms, halo, base_ref, pre_ref)

    @pl.when(parity[0] != 0)
    def _():
        for o in range(orbits):
            near = slice(o * atoms, o * atoms + halo)
            far = slice(o * atoms + halo, (o + 1) * atoms)
            back = got_i[o * halo : (o + 1) * halo, :].astype(F32)
            base_ref[near, :] = grown(local[near, :] + back, near)
            base_ref[far, :] = grown(local[far, :], far)
        if pre_ref is not None:
            pre_ref[...] = times(crosst, base_ref[...].astype(BF16))


def send_body(k, tail, parity, got_x, pre, gram, *refs):
    out = refs[-1]
    edge_size = pre.shape[0]
    factor = 1.0 if k == 0 else 2.0

    @pl.when(parity[0] == 0)
    def _():
        out[:edge_size, :] = (pre[...] + factor * got_x[:edge_size, :].astype(F32)).astype(BF16)

    @pl.when(parity[0] != 0)
    def _():
        out[:edge_size, :] = (pre[...] + factor * times(gram, got_x[:edge_size, :])).astype(BF16)

    if tail == "sum":
        table, got = refs[:-1]
        put_table(table[...] + get_table(got, edge_size), out, edge_size)
        blank(out, edge_size + TAIL)
    elif tail == "pass":
        out[edge_size : edge_size + TAIL, :] = refs[0][edge_size : edge_size + TAIL, :]
        blank(out, edge_size + TAIL)
    else:
        blank(out, edge_size)


def finish(atoms, orbits, halo, k, parity, got_x, base, cross, write):
    factor = 1.0 if k == 0 else 2.0

    @pl.when(parity[0] == 0)
    def _():
        for o in range(orbits):
            near = slice(o * atoms, o * atoms + halo)
            back = got_x[o * halo : (o + 1) * halo, :].astype(F32)
            write(o, 0, base[near, :] + factor * back)
            write(o, halo, base[o * atoms + halo : (o + 1) * atoms, :])

    @pl.when(parity[0] != 0)
    def _():
        total = base[...] + factor * times(cross, got_x[: orbits * halo, :])
        for o in range(orbits):
            write(o, 0, total[o * atoms : (o + 1) * atoms, :])


def next_body(atoms, orbits, halo, k, tail, scale, ride, parity, got_x, base, cross, crosst, _, *refs):
    keep = k < STEPS - 2
    outs = refs[len(refs) - 2 - keep - (tail == "start") :]
    (v_ref, w_ref, out) = outs[:3] if keep else (None, *outs)
    edge_size = orbits * halo

    def write(o, at, piece):
        rows = slice(o * atoms + at, o * atoms + at + piece.shape[0])
        if keep:
            v_ref[rows, :] = piece
        w_ref[rows, :] = piece.astype(BF16)

    finish(atoms, orbits, halo, k, parity, got_x, base, cross, write)

    @pl.when(parity[0] == 0)
    def _():
        out[:edge_size, :] = times(crosst, w_ref).astype(BF16)

    @pl.when(parity[0] != 0)
    def _():
        put_edge(atoms, halo, w_ref, out)

    if tail == "start":
        others = operands_of(HALF)[:-1]
        made = dots_of(HALF, refs[: len(others)] + (v_ref,))
        table = table_of(scale, made, refs[len(others) : len(others) + HALF - 1])
        outs[3][...] = table
        if ride:
            put_table(table, out, edge_size)
    elif tail == "pass":
        out[edge_size:, :] = got_x[edge_size : edge_size + TAIL, :]


def last_body(atoms, orbits, halo, k, turn, parity, got_x, base, cross, table, *refs):
    out, moments = refs[-2:]
    edge_size = orbits * halo

    def write(o, at, piece):
        rows = slice(o * atoms + at, o * atoms + at + piece.shape[0])
        out[pl.ds(at * orbits + o, piece.shape[0], stride=orbits) if turn else rows, :] = piece

    finish(atoms, orbits, halo, k, parity, got_x, base, cross, write)
    total = table[...]
    for got in refs[:-2]:
        total = total + get_table(got, edge_size)
    moments[...] = total[: STEPS + 1, :]


def per_device(probes, blocks, block_rows, block_cols, counts):
    atoms, orbits, width = probes.shape
    halo = atoms // 2
    size, edge_size = atoms * orbits, halo * orbits
    slots = blocks.shape[0]
    dims = (atoms, orbits, halo)
    turn = width == 128
    ring = lax.axis_size(RING)
    ride = ring == STEPS
    scale = 1.0 / (size * ring)
    parity = lax.axis_index("orb").astype(jnp.int32).reshape(1)
    between = [(i, (i + 1) % ring) for i in range(1, ring, 2)]
    between = between + [(b, a) for a, b in between]
    across = lambda x: lax.ppermute(x, RING, between)
    inside = lambda x: lax.ppermute(x, "orb", [(0, 1), (1, 0)])

    slot = jnp.arange(slots, dtype=jnp.int32)
    pair = jnp.where(slot < counts[0], block_cols * atoms + block_rows, -atoms)
    flat = blocks.transpose(1, 2, 0).reshape(orbits * orbits, slots)
    row_hot = pltpu.VMEM((atoms, slots), BF16)
    (crosst,) = call(
        functools.partial(cross_body, *dims),
        (((edge_size, size), BF16),),
        pair, flat,
        flops=2 * orbits * orbits * slots * atoms * halo,
        scratch=[pltpu.VMEM((orbits // 2, orbits * (halo + PAD), 2 * atoms), F32), row_hot],
        limit=24,
    )
    whole, rounded, message = ((size, width), F32), ((size, width), BF16), ((edge_size, width), BF16)
    longer = ((edge_size + TAIL, width), BF16)
    far_rows = [edge_size + LONGER + (TAIL if ride and k >= HALF else 0) for k in range(STEPS)]
    v, w, send_x, send_i = call(
        functools.partial(first_body, *dims, turn),
        (whole, rounded, ((far_rows[0], width), BF16), message),
        parity,
        (probes if turn else probes.transpose(1, 0, 2)).reshape(size, width),
        crosst,
        smem=1,
    )
    vectors, tables, got = [v], [], []
    for k in range(STEPS):
        got_x = across(send_x)
        if k > 0:
            tail = {HALF: "start", HALF + 2: "pass"}.get(k) if ride or k == HALF else None
            extra, outs = (), (whole, rounded, longer if tail and ride else message)[k == STEPS - 1 :]
            if k == HALF:
                extra, outs = (*(vectors[m] for m in operands_of(HALF)[:-1]), *tables), outs + (((ROWS, width), F32),)
            made = call(
                functools.partial(next_body, *dims, k - 1, tail, scale, ride),
                outs, parity, arrived, base, cross, crosst, send_x, *extra, smem=1,
            )
            if k < STEPS - 1:
                vectors.append(made[0])
            w, send_i = made[k < STEPS - 1 :][:2]
            if k == HALF:
                table = made[3]
        got_i = inside(send_i)
        if k == 0:
            own, cross, gram, local = call(
                functools.partial(own_body, *dims),
                (((size, size), BF16), ((size, edge_size), BF16), ((edge_size, edge_size), BF16), whole),
                pair, flat, crosst, w, send_i,
                scratch=[pltpu.VMEM((orbits // 2, orbits * (atoms + PAD), 2 * atoms), F32), row_hot],
                limit=24,
            )
        else:
            dots = (((len(DOTS[k]), width), F32),) if k < HALF else ()
            local, *made = call(
                functools.partial(local_body, k),
                (whole,) + dots,
                own, w, *((vectors[m] for m in operands_of(k)) if k < HALF else ()),
            )
            tables = tables + made
        base, *pre = call(
            functools.partial(before_body, *dims, k),
            (whole, ((edge_size, width), F32))[: 2 - (k == STEPS - 1)],
            parity, got_i, local, vectors[max(k - 1, 0)], cross, crosst, smem=1,
        )
        arrived = got_x
        if k < STEPS - 1:
            tail = {HALF: "sum", HALF + 2: "pass"}.get(k) if ride else None
            extra = {"sum": (table, got_i), "pass": (got_i,)}[tail] if tail else ()
            (send_x,) = call(
                functools.partial(send_body, k, tail),
                (((far_rows[k + 1], width), BF16),),
                parity, got_x, *pre, gram, *extra, smem=1,
            )
        if ride and k >= HALF:
            got.append(got_i if k % 2 == 0 else got_x)
    last, moments = call(
        functools.partial(last_body, *dims, STEPS - 1, turn),
        (whole, ((STEPS + 1, width), F32)),
        parity, got_x, base, cross, table, *got, smem=1,
    )
    last = last.reshape(atoms, orbits, width) if turn else last.reshape(orbits, atoms, width).transpose(1, 0, 2)
    return last, moments if ride else lax.psum(moments, RING)


def solution(mesh):
    in_specs = (
        P(("groups", "dom", "orb"), None, "probe"),
        P(("groups", "dom", "orb"), None, None),
        P(("groups", "dom", "orb")),
        P(("groups", "dom", "orb")),
        P(("groups", "dom", "orb")),
    )
    out_specs = (P(("groups", "dom", "orb"), None, "probe"), P("groups", "probe"))
    return jax.shard_map(
        per_device, mesh=mesh, in_specs=in_specs, out_specs=out_specs, check_vma=False
    )
```

```python
import functools

import jax
import jax.numpy as jnp
from jax import lax
from jax.experimental import pallas as pl
from jax.experimental.pallas import tpu as pltpu
from jax.sharding import PartitionSpec as P

STEPS = 8
HALF = STEPS // 2
RING = ("dom", "orb")
F32, BF16 = jnp.float32, jnp.bfloat16
VMEM = pl.BlockSpec(memory_space=pltpu.VMEM)
SMEM = pl.BlockSpec(memory_space=pltpu.SMEM)
NT = (((1,), (1,)), ((), ()))
AHEAD = 1_000_000_000
PAD = 8
ROWS = 16
TAIL = 3 * ROWS
LONGER = ROWS
DOTS = [[(0, n)] + [(m, n) for m in (n - 1, n) if m > 0 and HALF < m + n] for n in range(HALF + 1)]
DOTS[:2] = [[], DOTS[0] + DOTS[1]]


def operands_of(n):
    return sorted({m for pair in DOTS[n] for m in pair})


def call(body, outs, *operands, flops=0, scratch=(), smem=0, limit=16):
    size = sum(o.size * o.dtype.itemsize for o in operands)
    return pl.pallas_call(
        body,
        out_shape=tuple(jax.ShapeDtypeStruct(s, t) for s, t in outs),
        in_specs=[SMEM] * smem + [VMEM] * (len(operands) - smem),
        out_specs=(VMEM,) * len(outs),
        scratch_shapes=scratch,
        compiler_params=pltpu.CompilerParams(vmem_limit_bytes=limit << 20),
        cost_estimate=pl.CostEstimate(flops=flops, bytes_accessed=size, transcendentals=0) if flops else None,
    )(*operands)


def hot_body(atoms, pair, row_hot, col_ref):
    slots = pair.shape[0]
    pair_id = pair[...].reshape(1, slots)
    col_id = lax.div(pair_id, atoms)
    row_id = pair_id - col_id * atoms
    row_hot[...] = jnp.where(lax.broadcasted_iota(jnp.int32, (atoms, slots), 0) == row_id, 1.0, 0.0).astype(BF16)
    col_ref[...] = col_id


def place(atoms, orbits, first, total, row_hot, cols, blocks, target):
    col_id = cols[...]
    lanes = 2 * atoms
    lane = lax.broadcasted_iota(jnp.int32, (orbits, lanes), 1)

    def one(q, _):
        hot = []
        for n in range(4):
            here = jnp.where(col_id == first + 4 * q + n, 1.0, 0.0).astype(BF16)
            hot.append(row_hot[...] * here)
        hot = jnp.concatenate(hot, axis=0)
        tile = lax.dot_general(blocks[...], hot, NT, preferred_element_type=F32)
        for two in range(2):
            for i in range(0, orbits, 2):
                at = slice(two * lanes, (two + 1) * lanes)
                left = tile[i * orbits : (i + 1) * orbits, at]
                right = tile[(i + 1) * orbits : (i + 2) * orbits, at]
                low = jnp.where(lane < atoms, left, pltpu.roll(right, atoms, 1))
                high = jnp.where(lane < atoms, pltpu.roll(left, atoms, 1), right)
                col = 4 * q + 2 * two
                target[i // 2, pl.ds(col, orbits, stride=total + PAD), :] = low
                target[i // 2, pl.ds(col + 1, orbits, stride=total + PAD), :] = high
        return 0

    lax.fori_loop(0, total // 4, one, 0, unroll=total // 4)


def gather_rows(source, piece, total, orbitals):
    starts = [j * (total + PAD) for j in orbitals]
    return jnp.concatenate([source[piece, start : start + total, :] for start in starts], axis=0)


def cross_body(atoms, orbits, halo, row_hot, cols, blocks, crosst_ref, cross_f32):
    place(atoms, orbits, atoms, halo, row_hot, cols, blocks, cross_f32)
    lanes = 2 * atoms
    for p in range(orbits // 2):
        at = slice(p * lanes, (p + 1) * lanes)
        crosst_ref[:, at] = gather_rows(cross_f32, p, halo, range(orbits)).astype(BF16)


def own_body(atoms, orbits, halo, row_hot, cols, blocks, crosst, w, _, own_ref, cross_ref, gram_ref, local_ref, own_f32):
    place(atoms, orbits, 0, atoms, row_hot, cols, blocks, own_f32)
    gram_ref[...] = lax.dot_general(crosst[...], crosst[...], NT, preferred_element_type=F32).astype(BF16)
    lanes = 2 * atoms
    for p in range(orbits // 2):
        at = slice(p * lanes, (p + 1) * lanes)
        cross_ref[at, :] = crosst[:, at].astype(F32).T.astype(BF16)
        turned = gather_rows(own_f32, p, atoms, range(orbits)).T
        parts = []
        for n in range(orbits // 2):
            other = gather_rows(own_f32, n, atoms, (2 * p, 2 * p + 1))
            parts.append((other + turned[:, n * lanes : (n + 1) * lanes]).astype(BF16))
        mine = jnp.concatenate(parts, axis=1)
        own_ref[at, :] = mine
        local_ref[at, :] = times(mine, w)


def put_edge(atoms, halo, w, out):
    for o in range(w.shape[0] // atoms):
        out[o * halo : (o + 1) * halo, :] = w[o * atoms : o * atoms + halo, :]


def blank(out, start):
    out[start:, :] = jnp.zeros((out.shape[0] - start, out.shape[1]), out.dtype)


def times(left, right):
    return jnp.dot(left[...], right[...], preferred_element_type=F32)


def first_body(atoms, orbits, halo, turn, parity, probes, crosst, v_ref, w_ref, out_x, out_i):
    for o in range(orbits):
        rows = slice(o * atoms, (o + 1) * atoms)
        v = probes[pl.ds(o, atoms, stride=orbits), :] if turn else probes[rows, :]
        v_ref[rows, :] = v
        w_ref[rows, :] = v.astype(BF16)

    @pl.when(parity[0] == 0)
    def _():
        put_edge(atoms, halo, w_ref, out_x)
        out_i[...] = times(crosst, w_ref).astype(BF16)

    blank(out_x, orbits * halo)

    @pl.when(parity[0] != 0)
    def _():
        put_edge(atoms, halo, w_ref, out_i)
        out_x[: orbits * halo, :] = times(crosst, w_ref).astype(BF16)


def dots_of(n, refs):
    vectors = dict(zip(operands_of(n), refs))
    return [jnp.sum(vectors[a][...] * vectors[b][...], axis=0, keepdims=True) for a, b in DOTS[n]]


def local_body(k, own, w, *refs):
    refs[-1 if k >= HALF else -2][...] = times(own, w)
    if k < HALF:
        refs[-1][...] = jnp.concatenate(dots_of(k, refs), axis=0)


def table_of(scale, made, tables):
    dots = dict(zip(DOTS[HALF], made))
    for table, pairs in zip(tables, DOTS[1:]):
        dots.update({pair: table[n : n + 1, :] for n, pair in enumerate(pairs)})
    rows = [dots[0, n] for n in range(HALF + 1)]
    for n in range(HALF + 1, STEPS + 1):
        rows.append(2.0 * dots[n // 2, n - n // 2] - dots[0, n % 2])
    rows.append(jnp.zeros((ROWS - STEPS - 1, rows[0].shape[1]), F32))
    return jnp.concatenate(rows, axis=0) * scale


def put_table(table, out, start):
    for n in range(3):
        piece = table.astype(BF16)
        out[start + n * ROWS : start + (n + 1) * ROWS, :] = piece
        table = table - piece.astype(F32)


def get_table(got, start):
    pieces = [got[start + n * ROWS : start + (n + 1) * ROWS, :].astype(F32) for n in range(3)]
    return pieces[0] + (pieces[1] + pieces[2])


def before_body(atoms, orbits, halo, k, parity, got_i, local, previous, cross, crosst, base_ref, pre_ref=None):
    edge_size = orbits * halo
    grown = lambda total, rows: total if k == 0 else 2.0 * total - previous[rows, :]

    @pl.when(parity[0] == 0)
    def _():
        total = local[...] + times(cross, got_i[:edge_size, :])
        base_ref[...] = grown(total, slice(None))
        if pre_ref is not None:
            put_edge(atoms, halo, base_ref, pre_ref)

    @pl.when(parity[0] != 0)
    def _():
        for o in range(orbits):
            near = slice(o * atoms, o * atoms + halo)
            far = slice(o * atoms + halo, (o + 1) * atoms)
            back = got_i[o * halo : (o + 1) * halo, :].astype(F32)
            base_ref[near, :] = grown(local[near, :] + back, near)
            base_ref[far, :] = grown(local[far, :], far)
        if pre_ref is not None:
            pre_ref[...] = times(crosst, base_ref[...].astype(BF16))


def send_body(k, tail, parity, got_x, pre, gram, *refs):
    out = refs[-1]
    edge_size = pre.shape[0]
    factor = 1.0 if k == 0 else 2.0

    @pl.when(parity[0] == 0)
    def _():
        out[:edge_size, :] = (pre[...] + factor * got_x[:edge_size, :].astype(F32)).astype(BF16)

    @pl.when(parity[0] != 0)
    def _():
        out[:edge_size, :] = (pre[...] + factor * times(gram, got_x[:edge_size, :])).astype(BF16)

    if tail == "sum":
        table, got = refs[:-1]
        put_table(table[...] + get_table(got, edge_size), out, edge_size)
        blank(out, edge_size + TAIL)
    elif tail == "pass":
        out[edge_size : edge_size + TAIL, :] = refs[0][edge_size : edge_size + TAIL, :]
        blank(out, edge_size + TAIL)
    else:
        blank(out, edge_size)


def finish(atoms, orbits, halo, k, parity, got_x, base, cross, write):
    factor = 1.0 if k == 0 else 2.0

    @pl.when(parity[0] == 0)
    def _():
        for o in range(orbits):
            near = slice(o * atoms, o * atoms + halo)
            back = got_x[o * halo : (o + 1) * halo, :].astype(F32)
            write(o, 0, base[near, :] + factor * back)
            write(o, halo, base[o * atoms + halo : (o + 1) * atoms, :])

    @pl.when(parity[0] != 0)
    def _():
        total = base[...] + factor * times(cross, got_x[: orbits * halo, :])
        for o in range(orbits):
            write(o, 0, total[o * atoms : (o + 1) * atoms, :])


def next_body(atoms, orbits, halo, k, tail, scale, ride, parity, got_x, base, cross, crosst, _, *refs):
    keep = k < STEPS - 2
    outs = refs[len(refs) - 2 - keep - (tail == "start") :]
    (v_ref, w_ref, out) = outs[:3] if keep else (None, *outs)
    edge_size = orbits * halo

    def write(o, at, piece):
        rows = slice(o * atoms + at, o * atoms + at + piece.shape[0])
        if keep:
            v_ref[rows, :] = piece
        w_ref[rows, :] = piece.astype(BF16)

    finish(atoms, orbits, halo, k, parity, got_x, base, cross, write)

    @pl.when(parity[0] == 0)
    def _():
        out[:edge_size, :] = times(crosst, w_ref).astype(BF16)

    @pl.when(parity[0] != 0)
    def _():
        put_edge(atoms, halo, w_ref, out)

    if tail == "start":
        others = operands_of(HALF)[:-1]
        made = dots_of(HALF, refs[: len(others)] + (v_ref,))
        table = table_of(scale, made, refs[len(others) : len(others) + HALF - 1])
        outs[3][...] = table
        if ride:
            put_table(table, out, edge_size)
    elif tail == "pass":
        out[edge_size:, :] = got_x[edge_size : edge_size + TAIL, :]


def last_body(atoms, orbits, halo, k, turn, parity, got_x, base, cross, table, *refs):
    out, moments = refs[-2:]
    edge_size = orbits * halo

    def write(o, at, piece):
        rows = slice(o * atoms + at, o * atoms + at + piece.shape[0])
        out[pl.ds(at * orbits + o, piece.shape[0], stride=orbits) if turn else rows, :] = piece

    finish(atoms, orbits, halo, k, parity, got_x, base, cross, write)
    total = table[...]
    for got in refs[:-2]:
        total = total + get_table(got, edge_size)
    moments[...] = total[: STEPS + 1, :]


def per_device(probes, blocks, block_rows, block_cols, counts):
    atoms, orbits, width = probes.shape
    halo = atoms // 2
    size, edge_size = atoms * orbits, halo * orbits
    slots = blocks.shape[0]
    dims = (atoms, orbits, halo)
    turn = width == 128
    ring = lax.axis_size(RING)
    ride = ring == STEPS
    scale = 1.0 / (size * ring)
    parity = lax.axis_index("orb").astype(jnp.int32).reshape(1)
    between = [(i, (i + 1) % ring) for i in range(1, ring, 2)]
    between = between + [(b, a) for a, b in between]
    across = lambda x: lax.ppermute(x, RING, between)
    inside = lambda x: lax.ppermute(x, "orb", [(0, 1), (1, 0)])

    slot = jnp.arange(slots, dtype=jnp.int32)
    pair = jnp.where(slot < counts[0], block_cols * atoms + block_rows, -atoms)
    flat = blocks.transpose(1, 2, 0).reshape(orbits * orbits, slots)
    row_hot, cols = call(
        functools.partial(hot_body, atoms),
        (((atoms, slots), BF16), ((1, slots), jnp.int32)),
        pair,
        flops=AHEAD,
    )
    (crosst,) = call(
        functools.partial(cross_body, *dims),
        (((edge_size, size), BF16),),
        row_hot, cols, flat,
        flops=2 * orbits * orbits * slots * atoms * halo,
        scratch=[pltpu.VMEM((orbits // 2, orbits * (halo + PAD), 2 * atoms), F32)],
        limit=24,
    )
    whole, rounded, message = ((size, width), F32), ((size, width), BF16), ((edge_size, width), BF16)
    longer = ((edge_size + TAIL, width), BF16)
    far_rows = [edge_size + LONGER + (TAIL if ride and k >= HALF else 0) for k in range(STEPS)]
    v, w, send_x, send_i = call(
        functools.partial(first_body, *dims, turn),
        (whole, rounded, ((far_rows[0], width), BF16), message),
        parity,
        (probes if turn else probes.transpose(1, 0, 2)).reshape(size, width),
        crosst,
        smem=1,
    )
    vectors, tables, got = [v], [], []
    for k in range(STEPS):
        got_x = across(send_x)
        if k > 0:
            tail = {HALF: "start", HALF + 2: "pass"}.get(k) if ride or k == HALF else None
            extra, outs = (), (whole, rounded, longer if tail and ride else message)[k == STEPS - 1 :]
            if k == HALF:
                extra, outs = (*(vectors[m] for m in operands_of(HALF)[:-1]), *tables), outs + (((ROWS, width), F32),)
            made = call(
                functools.partial(next_body, *dims, k - 1, tail, scale, ride),
                outs, parity, arrived, base, cross, crosst, send_x, *extra, smem=1,
            )
            if k < STEPS - 1:
                vectors.append(made[0])
            w, send_i = made[k < STEPS - 1 :][:2]
            if k == HALF:
                table = made[3]
        got_i = inside(send_i)
        if k == 0:
            own, cross, gram, local = call(
                functools.partial(own_body, *dims),
                (((size, size), BF16), ((size, edge_size), BF16), ((edge_size, edge_size), BF16), whole),
                row_hot, cols, flat, crosst, w, send_i,
                scratch=[pltpu.VMEM((orbits // 2, orbits * (atoms + PAD), 2 * atoms), F32)],
                limit=24,
            )
        else:
            dots = (((len(DOTS[k]), width), F32),) if k < HALF else ()
            local, *made = call(
                functools.partial(local_body, k),
                (whole,) + dots,
                own, w, *((vectors[m] for m in operands_of(k)) if k < HALF else ()),
            )
            tables = tables + made
        base, *pre = call(
            functools.partial(before_body, *dims, k),
            (whole, ((edge_size, width), F32))[: 2 - (k == STEPS - 1)],
            parity, got_i, local, vectors[max(k - 1, 0)], cross, crosst, smem=1,
        )
        arrived = got_x
        if k < STEPS - 1:
            tail = {HALF: "sum", HALF + 2: "pass"}.get(k) if ride else None
            extra = {"sum": (table, got_i), "pass": (got_i,)}[tail] if tail else ()
            (send_x,) = call(
                functools.partial(send_body, k, tail),
                (((far_rows[k + 1], width), BF16),),
                parity, got_x, *pre, gram, *extra, smem=1,
            )
        if ride and k >= HALF:
            got.append(got_i if k % 2 == 0 else got_x)
    last, moments = call(
        functools.partial(last_body, *dims, STEPS - 1, turn),
        (whole, ((STEPS + 1, width), F32)),
        parity, got_x, base, cross, table, *got, smem=1,
    )
    last = last.reshape(atoms, orbits, width) if turn else last.reshape(orbits, atoms, width).transpose(1, 0, 2)
    return last, moments if ride else lax.psum(moments, RING)


def solution(mesh):
    in_specs = (
        P(("groups", "dom", "orb"), None, "probe"),
        P(("groups", "dom", "orb"), None, None),
        P(("groups", "dom", "orb")),
        P(("groups", "dom", "orb")),
        P(("groups", "dom", "orb")),
    )
    out_specs = (P(("groups", "dom", "orb"), None, "probe"), P("groups", "probe"))
    return jax.shard_map(
        per_device, mesh=mesh, in_specs=in_specs, out_specs=out_specs, check_vma=False
    )
```

```python
import functools

import jax
import jax.numpy as jnp
from jax import lax
from jax.experimental import pallas as pl
from jax.experimental.pallas import tpu as pltpu
from jax.sharding import PartitionSpec as P

STEPS = 8
HALF = STEPS // 2
RING = ("dom", "orb")
F32, BF16 = jnp.float32, jnp.bfloat16
VMEM = pl.BlockSpec(memory_space=pltpu.VMEM)
SMEM = pl.BlockSpec(memory_space=pltpu.SMEM)
NT = (((1,), (1,)), ((), ()))
AHEAD = 1_000_000_000
PAD = 8
ROWS = STEPS + 1
LONGER = 16
TAIL = -(-3 * ROWS // 16) * 16
DOTS = [[(0, n)] + [(m, n) for m in (n - 1, n) if m > 0 and HALF < m + n] for n in range(HALF + 1)]
DOTS[:2] = [[], DOTS[0] + DOTS[1]]


def operands_of(n):
    return sorted({m for pair in DOTS[n] for m in pair})


def call(body, outs, *operands, flops=0, scratch=(), smem=0, limit=16):
    size = sum(o.size * o.dtype.itemsize for o in operands)
    return pl.pallas_call(
        body,
        out_shape=tuple(jax.ShapeDtypeStruct(s, t) for s, t in outs),
        in_specs=[SMEM] * smem + [VMEM] * (len(operands) - smem),
        out_specs=(VMEM,) * len(outs),
        scratch_shapes=scratch,
        compiler_params=pltpu.CompilerParams(vmem_limit_bytes=limit << 20),
        cost_estimate=pl.CostEstimate(flops=flops, bytes_accessed=size, transcendentals=0) if flops else None,
    )(*operands)


def hot_body(atoms, pair, row_hot, col_ref):
    slots = pair.shape[0]
    pair_id = pair[...].reshape(1, slots)
    col_id = lax.div(pair_id, atoms)
    row_id = pair_id - col_id * atoms
    row_hot[...] = jnp.where(lax.broadcasted_iota(jnp.int32, (atoms, slots), 0) == row_id, 1.0, 0.0).astype(BF16)
    col_ref[...] = col_id


def place(atoms, orbits, first, total, row_hot, cols, blocks, target):
    col_id = cols[...]
    lanes = 2 * atoms
    lane = lax.broadcasted_iota(jnp.int32, (orbits, lanes), 1)

    def one(q, _):
        hot = []
        for n in range(4):
            here = jnp.where(col_id == first + 4 * q + n, 1.0, 0.0).astype(BF16)
            hot.append(row_hot[...] * here)
        hot = jnp.concatenate(hot, axis=0)
        tile = lax.dot_general(blocks[...], hot, NT, preferred_element_type=F32)
        for two in range(2):
            for i in range(0, orbits, 2):
                at = slice(two * lanes, (two + 1) * lanes)
                left = tile[i * orbits : (i + 1) * orbits, at]
                right = tile[(i + 1) * orbits : (i + 2) * orbits, at]
                low = jnp.where(lane < atoms, left, pltpu.roll(right, atoms, 1))
                high = jnp.where(lane < atoms, pltpu.roll(left, atoms, 1), right)
                col = 4 * q + 2 * two
                target[i // 2, pl.ds(col, orbits, stride=total + PAD), :] = low
                target[i // 2, pl.ds(col + 1, orbits, stride=total + PAD), :] = high
        return 0

    lax.fori_loop(0, total // 4, one, 0, unroll=total // 4)


def gather_rows(source, piece, total, orbitals):
    starts = [j * (total + PAD) for j in orbitals]
    return jnp.concatenate([source[piece, start : start + total, :] for start in starts], axis=0)


def cross_body(atoms, orbits, halo, row_hot, cols, blocks, crosst_ref, cross_f32):
    place(atoms, orbits, atoms, halo, row_hot, cols, blocks, cross_f32)
    lanes = 2 * atoms
    for p in range(orbits // 2):
        at = slice(p * lanes, (p + 1) * lanes)
        crosst_ref[:, at] = gather_rows(cross_f32, p, halo, range(orbits)).astype(BF16)


def own_body(atoms, orbits, halo, row_hot, cols, blocks, crosst, w, _, own_ref, cross_ref, gram_ref, local_ref, own_f32):
    place(atoms, orbits, 0, atoms, row_hot, cols, blocks, own_f32)
    gram_ref[...] = lax.dot_general(crosst[...], crosst[...], NT, preferred_element_type=F32).astype(BF16)
    lanes = 2 * atoms
    for p in range(orbits // 2):
        at = slice(p * lanes, (p + 1) * lanes)
        cross_ref[at, :] = crosst[:, at].astype(F32).T.astype(BF16)
        turned = gather_rows(own_f32, p, atoms, range(orbits)).T
        parts = []
        for n in range(orbits // 2):
            other = gather_rows(own_f32, n, atoms, (2 * p, 2 * p + 1))
            parts.append((other + turned[:, n * lanes : (n + 1) * lanes]).astype(BF16))
        mine = jnp.concatenate(parts, axis=1)
        own_ref[at, :] = mine
        local_ref[at, :] = times(mine, w)


def put_edge(atoms, halo, w, out):
    for o in range(w.shape[0] // atoms):
        out[o * halo : (o + 1) * halo, :] = w[o * atoms : o * atoms + halo, :]


def blank(out, start):
    if start < out.shape[0]:
        out[start:, :] = jnp.zeros((out.shape[0] - start, out.shape[1]), out.dtype)


def times(left, right):
    return jnp.dot(left[...], right[...], preferred_element_type=F32)


def first_body(atoms, orbits, halo, turn, parity, probes, crosst, v_ref, w_ref, out_x, out_i):
    for o in range(orbits):
        rows = slice(o * atoms, (o + 1) * atoms)
        v = probes[pl.ds(o, atoms, stride=orbits), :] if turn else probes[rows, :]
        v_ref[rows, :] = v
        w_ref[rows, :] = v.astype(BF16)

    @pl.when(parity[0] == 0)
    def _():
        put_edge(atoms, halo, w_ref, out_x)
        out_i[...] = times(crosst, w_ref).astype(BF16)

    blank(out_x, orbits * halo)

    @pl.when(parity[0] != 0)
    def _():
        put_edge(atoms, halo, w_ref, out_i)
        out_x[: orbits * halo, :] = times(crosst, w_ref).astype(BF16)


def dots_of(n, refs):
    vectors = dict(zip(operands_of(n), refs))
    return [jnp.sum(vectors[a][...] * vectors[b][...], axis=0, keepdims=True) for a, b in DOTS[n]]


def local_body(k, own, w, *refs):
    refs[-1 if k >= HALF else -2][...] = times(own, w)
    if k < HALF:
        refs[-1][...] = jnp.concatenate(dots_of(k, refs), axis=0)


def table_of(scale, made, tables):
    dots = dict(zip(DOTS[HALF], made))
    for table, pairs in zip(tables, DOTS[1:]):
        dots.update({pair: table[n : n + 1, :] for n, pair in enumerate(pairs)})
    rows = [dots[0, n] for n in range(HALF + 1)]
    for n in range(HALF + 1, STEPS + 1):
        rows.append(2.0 * dots[n // 2, n - n // 2] - dots[0, n % 2])
    return jnp.concatenate(rows, axis=0) * scale


def put_table(table, out, start):
    pieces = []
    for _ in range(3):
        pieces.append(table.astype(BF16).astype(F32))
        table = table - pieces[-1]
    pieces.append(jnp.zeros((TAIL - 3 * ROWS, table.shape[1]), F32))
    out[start : start + TAIL, :] = jnp.concatenate(pieces, axis=0).astype(BF16)


def get_table(got, start):
    pieces = got[start : start + TAIL, :].astype(F32)
    return pieces[:ROWS] + (pieces[ROWS : 2 * ROWS] + pieces[2 * ROWS : 3 * ROWS])


def before_body(atoms, orbits, halo, k, parity, got_i, local, previous, cross, crosst, base_ref, pre_ref=None):
    edge_size = orbits * halo
    grown = lambda total, rows: total if k == 0 else 2.0 * total - previous[rows, :]

    @pl.when(parity[0] == 0)
    def _():
        total = local[...] + times(cross, got_i[:edge_size, :])
        base_ref[...] = grown(total, slice(None))
        if pre_ref is not None:
            put_edge(atoms, halo, base_ref, pre_ref)

    @pl.when(parity[0] != 0)
    def _():
        for o in range(orbits):
            near = slice(o * atoms, o * atoms + halo)
            far = slice(o * atoms + halo, (o + 1) * atoms)
            back = got_i[o * halo : (o + 1) * halo, :].astype(F32)
            base_ref[near, :] = grown(local[near, :] + back, near)
            base_ref[far, :] = grown(local[far, :], far)
        if pre_ref is not None:
            pre_ref[...] = times(crosst, base_ref[...].astype(BF16))


def send_body(k, tail, parity, got_x, pre, gram, *refs):
    out = refs[-1]
    edge_size = pre.shape[0]
    factor = 1.0 if k == 0 else 2.0

    @pl.when(parity[0] == 0)
    def _():
        out[:edge_size, :] = (pre[...] + factor * got_x[:edge_size, :].astype(F32)).astype(BF16)

    @pl.when(parity[0] != 0)
    def _():
        out[:edge_size, :] = (pre[...] + factor * times(gram, got_x[:edge_size, :])).astype(BF16)

    if tail == "sum":
        table, got = refs[:-1]
        put_table(table[...] + get_table(got, edge_size), out, edge_size)
        blank(out, edge_size + TAIL)
    elif tail == "pass":
        out[edge_size : edge_size + TAIL, :] = refs[0][edge_size : edge_size + TAIL, :]
        blank(out, edge_size + TAIL)
    else:
        blank(out, edge_size)


def finish(atoms, orbits, halo, k, parity, got_x, base, cross, write):
    factor = 1.0 if k == 0 else 2.0

    @pl.when(parity[0] == 0)
    def _():
        for o in range(orbits):
            near = slice(o * atoms, o * atoms + halo)
            back = got_x[o * halo : (o + 1) * halo, :].astype(F32)
            write(o, 0, base[near, :] + factor * back)
            write(o, halo, base[o * atoms + halo : (o + 1) * atoms, :])

    @pl.when(parity[0] != 0)
    def _():
        total = base[...] + factor * times(cross, got_x[: orbits * halo, :])
        for o in range(orbits):
            write(o, 0, total[o * atoms : (o + 1) * atoms, :])


def next_body(atoms, orbits, halo, k, tail, scale, ride, parity, got_x, base, cross, crosst, _, *refs):
    keep = k < STEPS - 2
    outs = refs[len(refs) - 2 - keep - (tail == "start") :]
    (v_ref, w_ref, out) = outs[:3] if keep else (None, *outs)
    edge_size = orbits * halo

    def write(o, at, piece):
        rows = slice(o * atoms + at, o * atoms + at + piece.shape[0])
        if keep:
            v_ref[rows, :] = piece
        w_ref[rows, :] = piece.astype(BF16)

    finish(atoms, orbits, halo, k, parity, got_x, base, cross, write)

    @pl.when(parity[0] == 0)
    def _():
        out[:edge_size, :] = times(crosst, w_ref).astype(BF16)

    @pl.when(parity[0] != 0)
    def _():
        put_edge(atoms, halo, w_ref, out)

    if tail == "start":
        others = operands_of(HALF)[:-1]
        made = dots_of(HALF, refs[: len(others)] + (v_ref,))
        table = table_of(scale, made, refs[len(others) : len(others) + HALF - 1])
        outs[3][...] = table
        if ride:
            put_table(table, out, edge_size)
    elif tail == "pass":
        out[edge_size:, :] = got_x[edge_size : edge_size + TAIL, :]


def last_body(atoms, orbits, halo, k, turn, parity, got_x, base, cross, table, *refs):
    out, moments = refs[-2:]
    edge_size = orbits * halo

    def write(o, at, piece):
        rows = slice(o * atoms + at, o * atoms + at + piece.shape[0])
        out[pl.ds(at * orbits + o, piece.shape[0], stride=orbits) if turn else rows, :] = piece

    finish(atoms, orbits, halo, k, parity, got_x, base, cross, write)
    total = table[...]
    for got in refs[:-2]:
        total = total + get_table(got, edge_size)
    moments[...] = total


def per_device(probes, blocks, block_rows, block_cols, counts):
    atoms, orbits, width = probes.shape
    halo = atoms // 2
    size, edge_size = atoms * orbits, halo * orbits
    slots = blocks.shape[0]
    dims = (atoms, orbits, halo)
    turn = width == 128
    ring = lax.axis_size(RING)
    ride = ring == STEPS
    scale = 1.0 / (size * ring)
    parity = lax.axis_index("orb").astype(jnp.int32).reshape(1)
    between = [(i, (i + 1) % ring) for i in range(1, ring, 2)]
    between = between + [(b, a) for a, b in between]
    across = lambda x: lax.ppermute(x, RING, between)
    inside = lambda x: lax.ppermute(x, "orb", [(0, 1), (1, 0)])

    slot = jnp.arange(slots, dtype=jnp.int32)
    pair = jnp.where(slot < counts[0], block_cols * atoms + block_rows, -atoms)
    flat = blocks.transpose(1, 2, 0).reshape(orbits * orbits, slots)
    row_hot, cols = call(
        functools.partial(hot_body, atoms),
        (((atoms, slots), BF16), ((1, slots), jnp.int32)),
        pair,
        flops=AHEAD,
    )
    (crosst,) = call(
        functools.partial(cross_body, *dims),
        (((edge_size, size), BF16),),
        row_hot, cols, flat,
        flops=2 * orbits * orbits * slots * atoms * halo,
        scratch=[pltpu.VMEM((orbits // 2, orbits * (halo + PAD), 2 * atoms), F32)],
        limit=24,
    )
    whole, rounded, message = ((size, width), F32), ((size, width), BF16), ((edge_size, width), BF16)
    longer = ((edge_size + TAIL, width), BF16)
    riding = [ride and k >= HALF for k in range(STEPS)]
    far_rows = [edge_size + (TAIL if riding[k] else 0) + (0 if riding[k] and k % 2 else LONGER) for k in range(STEPS)]
    v, w, send_x, send_i = call(
        functools.partial(first_body, *dims, turn),
        (whole, rounded, ((far_rows[0], width), BF16), message),
        parity,
        (probes if turn else probes.transpose(1, 0, 2)).reshape(size, width),
        crosst,
        smem=1,
    )
    vectors, tables, got = [v], [], []
    for k in range(STEPS):
        got_x = across(send_x)
        if k > 0:
            tail = {HALF: "start", HALF + 2: "pass"}.get(k) if ride or k == HALF else None
            extra, outs = (), (whole, rounded, longer if tail and ride else message)[k == STEPS - 1 :]
            if k == HALF:
                extra, outs = (*(vectors[m] for m in operands_of(HALF)[:-1]), *tables), outs + (((ROWS, width), F32),)
            made = call(
                functools.partial(next_body, *dims, k - 1, tail, scale, ride),
                outs, parity, arrived, base, cross, crosst, send_x, *extra, smem=1,
            )
            if k < STEPS - 1:
                vectors.append(made[0])
            w, send_i = made[k < STEPS - 1 :][:2]
            if k == HALF:
                table = made[3]
        got_i = inside(send_i)
        if k == 0:
            own, cross, gram, local = call(
                functools.partial(own_body, *dims),
                (((size, size), BF16), ((size, edge_size), BF16), ((edge_size, edge_size), BF16), whole),
                row_hot, cols, flat, crosst, w, send_i,
                scratch=[pltpu.VMEM((orbits // 2, orbits * (atoms + PAD), 2 * atoms), F32)],
                limit=24,
            )
        else:
            dots = (((len(DOTS[k]), width), F32),) if k < HALF else ()
            local, *made = call(
                functools.partial(local_body, k),
                (whole,) + dots,
                own, w, *((vectors[m] for m in operands_of(k)) if k < HALF else ()),
            )
            tables = tables + made
        base, *pre = call(
            functools.partial(before_body, *dims, k),
            (whole, ((edge_size, width), F32))[: 2 - (k == STEPS - 1)],
            parity, got_i, local, vectors[max(k - 1, 0)], cross, crosst, smem=1,
        )
        arrived = got_x
        if k < STEPS - 1:
            tail = {HALF: "sum", HALF + 2: "pass"}.get(k) if ride else None
            extra = {"sum": (table, got_i), "pass": (got_i,)}[tail] if tail else ()
            (send_x,) = call(
                functools.partial(send_body, k, tail),
                (((far_rows[k + 1], width), BF16),),
                parity, got_x, *pre, gram, *extra, smem=1,
            )
        if ride and k >= HALF:
            got.append(got_i if k % 2 == 0 else got_x)
    last, moments = call(
        functools.partial(last_body, *dims, STEPS - 1, turn),
        (whole, ((STEPS + 1, width), F32)),
        parity, got_x, base, cross, table, *got, smem=1,
    )
    last = last.reshape(atoms, orbits, width) if turn else last.reshape(orbits, atoms, width).transpose(1, 0, 2)
    return last, moments if ride else lax.psum(moments, RING)


def solution(mesh):
    in_specs = (
        P(("groups", "dom", "orb"), None, "probe"),
        P(("groups", "dom", "orb"), None, None),
        P(("groups", "dom", "orb")),
        P(("groups", "dom", "orb")),
        P(("groups", "dom", "orb")),
    )
    out_specs = (P(("groups", "dom", "orb"), None, "probe"), P("groups", "probe"))
    return jax.shard_map(
        per_device, mesh=mesh, in_specs=in_specs, out_specs=out_specs, check_vma=False
    )
```

```python
import functools

import jax
import jax.numpy as jnp
from jax import lax
from jax.experimental import pallas as pl
from jax.experimental.pallas import tpu as pltpu
from jax.sharding import PartitionSpec as P

STEPS = 8
HALF = STEPS // 2
RING = ("dom", "orb")
F32, BF16 = jnp.float32, jnp.bfloat16
VMEM = pl.BlockSpec(memory_space=pltpu.VMEM)
SMEM = pl.BlockSpec(memory_space=pltpu.SMEM)
NT = (((1,), (1,)), ((), ()))
AHEAD = 1_000_000_000
PAD = 8
ROWS = STEPS + 1
LONGER = 16
TAIL = -(-3 * ROWS // 16) * 16
DOTS = [[(0, n)] + [(m, n) for m in (n - 1, n) if m > 0 and HALF < m + n] for n in range(HALF + 1)]
DOTS[:2] = [[], DOTS[0] + DOTS[1]]


def operands_of(n):
    return sorted({m for pair in DOTS[n] for m in pair})


def call(body, outs, *operands, flops=0, scratch=(), smem=0, limit=16):
    size = sum(o.size * o.dtype.itemsize for o in operands)
    return pl.pallas_call(
        body,
        out_shape=tuple(jax.ShapeDtypeStruct(s, t) for s, t in outs),
        in_specs=[SMEM] * smem + [VMEM] * (len(operands) - smem),
        out_specs=(VMEM,) * len(outs),
        scratch_shapes=scratch,
        compiler_params=pltpu.CompilerParams(vmem_limit_bytes=limit << 20),
        cost_estimate=pl.CostEstimate(flops=flops, bytes_accessed=size, transcendentals=0) if flops else None,
    )(*operands)


def hot_body(atoms, pair, row_hot, col_ref):
    slots = pair.shape[0]
    pair_id = pair[...].reshape(1, slots)
    col_id = lax.div(pair_id, atoms)
    row_id = pair_id - col_id * atoms
    row_hot[...] = jnp.where(lax.broadcasted_iota(jnp.int32, (atoms, slots), 0) == row_id, 1.0, 0.0).astype(BF16)
    col_ref[...] = col_id


def place(atoms, orbits, first, total, row_hot, cols, blocks, target):
    col_id = cols[...]
    lanes = 2 * atoms
    lane = lax.broadcasted_iota(jnp.int32, (orbits, lanes), 1)

    def one(q, _):
        hot = []
        for n in range(4):
            here = jnp.where(col_id == first + 4 * q + n, 1.0, 0.0).astype(BF16)
            hot.append(row_hot[...] * here)
        hot = jnp.concatenate(hot, axis=0)
        tile = lax.dot_general(blocks[...], hot, NT, preferred_element_type=F32)
        for two in range(2):
            for i in range(0, orbits, 2):
                at = slice(two * lanes, (two + 1) * lanes)
                left = tile[i * orbits : (i + 1) * orbits, at]
                right = tile[(i + 1) * orbits : (i + 2) * orbits, at]
                low = jnp.where(lane < atoms, left, pltpu.roll(right, atoms, 1))
                high = jnp.where(lane < atoms, pltpu.roll(left, atoms, 1), right)
                col = 4 * q + 2 * two
                target[i // 2, pl.ds(col, orbits, stride=total + PAD), :] = low
                target[i // 2, pl.ds(col + 1, orbits, stride=total + PAD), :] = high
        return 0

    lax.fori_loop(0, total // 4, one, 0, unroll=total // 4)


def gather_rows(source, piece, total, orbitals):
    starts = [j * (total + PAD) for j in orbitals]
    return jnp.concatenate([source[piece, start : start + total, :] for start in starts], axis=0)


def cross_body(atoms, orbits, halo, row_hot, cols, blocks, crosst_ref, cross_f32):
    place(atoms, orbits, atoms, halo, row_hot, cols, blocks, cross_f32)
    lanes = 2 * atoms
    for p in range(orbits // 2):
        at = slice(p * lanes, (p + 1) * lanes)
        crosst_ref[:, at] = gather_rows(cross_f32, p, halo, range(orbits)).astype(BF16)


def own_body(atoms, orbits, halo, row_hot, cols, blocks, crosst, w, _, own_ref, cross_ref, gram_ref, local_ref, own_f32):
    place(atoms, orbits, 0, atoms, row_hot, cols, blocks, own_f32)
    gram_ref[...] = lax.dot_general(crosst[...], crosst[...], NT, preferred_element_type=F32).astype(BF16)
    lanes = 2 * atoms
    for p in range(orbits // 2):
        at = slice(p * lanes, (p + 1) * lanes)
        cross_ref[at, :] = crosst[:, at].astype(F32).T.astype(BF16)
        turned = gather_rows(own_f32, p, atoms, range(orbits)).T
        parts = []
        for n in range(orbits // 2):
            other = gather_rows(own_f32, n, atoms, (2 * p, 2 * p + 1))
            parts.append((other + turned[:, n * lanes : (n + 1) * lanes]).astype(BF16))
        mine = jnp.concatenate(parts, axis=1)
        own_ref[at, :] = mine
        local_ref[at, :] = times(mine, w)


def put_edge(atoms, halo, w, out):
    for o in range(w.shape[0] // atoms):
        out[o * halo : (o + 1) * halo, :] = w[o * atoms : o * atoms + halo, :]


def blank(out, start):
    if start < out.shape[0]:
        out[start:, :] = jnp.zeros((out.shape[0] - start, out.shape[1]), out.dtype)


def times(left, right):
    return jnp.dot(left[...], right[...], preferred_element_type=F32)


def first_body(atoms, orbits, halo, turn, parity, probes, crosst, v_ref, w_ref, out_x, out_i):
    for o in range(orbits):
        rows = slice(o * atoms, (o + 1) * atoms)
        v = probes[pl.ds(o, atoms, stride=orbits), :] if turn else probes[rows, :]
        v_ref[rows, :] = v
        w_ref[rows, :] = v.astype(BF16)

    @pl.when(parity[0] == 0)
    def _():
        put_edge(atoms, halo, w_ref, out_x)
        out_i[...] = times(crosst, w_ref).astype(BF16)

    blank(out_x, orbits * halo)

    @pl.when(parity[0] != 0)
    def _():
        put_edge(atoms, halo, w_ref, out_i)
        out_x[: orbits * halo, :] = times(crosst, w_ref).astype(BF16)


def dots_of(n, refs):
    vectors = dict(zip(operands_of(n), refs))
    return [jnp.sum(vectors[a][...] * vectors[b][...], axis=0, keepdims=True) for a, b in DOTS[n]]


def local_body(k, own, w, *refs):
    refs[-1 if k >= HALF else -2][...] = times(own, w)
    if k < HALF:
        refs[-1][...] = jnp.concatenate(dots_of(k, refs), axis=0)


def table_of(scale, made, tables):
    dots = dict(zip(DOTS[HALF], made))
    for table, pairs in zip(tables, DOTS[1:]):
        dots.update({pair: table[n : n + 1, :] for n, pair in enumerate(pairs)})
    rows = [dots[0, n] for n in range(HALF + 1)]
    for n in range(HALF + 1, STEPS + 1):
        rows.append(2.0 * dots[n // 2, n - n // 2] - dots[0, n % 2])
    return jnp.concatenate(rows, axis=0) * scale


def put_table(table, out, start):
    pieces = []
    for _ in range(3):
        pieces.append(table.astype(BF16).astype(F32))
        table = table - pieces[-1]
    pieces.append(jnp.zeros((TAIL - 3 * ROWS, table.shape[1]), F32))
    out[start : start + TAIL, :] = jnp.concatenate(pieces, axis=0).astype(BF16)


def get_table(got, start):
    pieces = got[start : start + TAIL, :].astype(F32)
    return pieces[:ROWS] + (pieces[ROWS : 2 * ROWS] + pieces[2 * ROWS : 3 * ROWS])


def before_body(atoms, orbits, halo, k, parity, got_i, local, previous, cross, crosst, base_ref, pre_ref=None):
    edge_size = orbits * halo
    grown = lambda total, rows: total if k == 0 else 2.0 * total - previous[rows, :]

    @pl.when(parity[0] == 0)
    def _():
        total = local[...] + times(cross, got_i[:edge_size, :])
        base_ref[...] = grown(total, slice(None))
        if pre_ref is not None:
            put_edge(atoms, halo, base_ref, pre_ref)

    @pl.when(parity[0] != 0)
    def _():
        for o in range(orbits):
            near = slice(o * atoms, o * atoms + halo)
            far = slice(o * atoms + halo, (o + 1) * atoms)
            back = got_i[o * halo : (o + 1) * halo, :].astype(F32)
            base_ref[near, :] = grown(local[near, :] + back, near)
            base_ref[far, :] = grown(local[far, :], far)
        if pre_ref is not None:
            pre_ref[...] = times(crosst, base_ref[...].astype(BF16))


def send_body(k, tail, parity, got_x, pre, gram, *refs):
    out = refs[-1]
    edge_size = pre.shape[0]
    factor = 1.0 if k == 0 else 2.0

    @pl.when(parity[0] == 0)
    def _():
        out[:edge_size, :] = (pre[...] + factor * got_x[:edge_size, :].astype(F32)).astype(BF16)

    @pl.when(parity[0] != 0)
    def _():
        out[:edge_size, :] = (pre[...] + factor * times(gram, got_x[:edge_size, :])).astype(BF16)

    if tail == "sum":
        table, got = refs[:-1]
        put_table(table[...] + get_table(got, edge_size), out, edge_size)
        blank(out, edge_size + TAIL)
    elif tail == "pass":
        out[edge_size : edge_size + TAIL, :] = refs[0][edge_size : edge_size + TAIL, :]
        blank(out, edge_size + TAIL)
    else:
        blank(out, edge_size)


def finish(atoms, orbits, halo, k, parity, got_x, base, cross, write):
    factor = 1.0 if k == 0 else 2.0

    @pl.when(parity[0] == 0)
    def _():
        for o in range(orbits):
            near = slice(o * atoms, o * atoms + halo)
            back = got_x[o * halo : (o + 1) * halo, :].astype(F32)
            write(o, 0, base[near, :] + factor * back)
            write(o, halo, base[o * atoms + halo : (o + 1) * atoms, :])

    @pl.when(parity[0] != 0)
    def _():
        total = base[...] + factor * times(cross, got_x[: orbits * halo, :])
        for o in range(orbits):
            write(o, 0, total[o * atoms : (o + 1) * atoms, :])


def next_body(atoms, orbits, halo, k, tail, scale, ride, parity, got_x, base, cross, crosst, _, *refs):
    keep = k < STEPS - 2
    outs = refs[len(refs) - 2 - keep - (tail == "start") :]
    (v_ref, w_ref, out) = outs[:3] if keep else (None, *outs)
    edge_size = orbits * halo

    def write(o, at, piece):
        rows = slice(o * atoms + at, o * atoms + at + piece.shape[0])
        if keep:
            v_ref[rows, :] = piece
        w_ref[rows, :] = piece.astype(BF16)

    finish(atoms, orbits, halo, k, parity, got_x, base, cross, write)

    @pl.when(parity[0] == 0)
    def _():
        out[:edge_size, :] = times(crosst, w_ref).astype(BF16)

    @pl.when(parity[0] != 0)
    def _():
        put_edge(atoms, halo, w_ref, out)

    if tail == "start":
        others = operands_of(HALF)[:-1]
        made = dots_of(HALF, refs[: len(others)] + (v_ref,))
        table = table_of(scale, made, refs[len(others) : len(others) + HALF - 1])
        outs[3][...] = table
        if ride:
            put_table(table, out, edge_size)
    elif tail == "pass":
        out[edge_size:, :] = got_x[edge_size : edge_size + TAIL, :]


def last_body(atoms, orbits, halo, k, turn, parity, got_x, base, cross, table, *refs):
    out, moments = refs[-2:]
    edge_size = orbits * halo

    def write(o, at, piece):
        rows = slice(o * atoms + at, o * atoms + at + piece.shape[0])
        out[pl.ds(at * orbits + o, piece.shape[0], stride=orbits) if turn else rows, :] = piece

    finish(atoms, orbits, halo, k, parity, got_x, base, cross, write)
    total = table[...]
    for got in refs[:-2]:
        total = total + get_table(got, edge_size)
    moments[...] = total


def halves_body(atoms, orbits, halo, parity, got_x, base, cross, table, *refs):
    *got, out, moments, full = refs
    edge_size = orbits * halo
    near = pl.program_id(0) == 1

    def put(at, make):
        for o in range(orbits):
            out[pl.ds(o, halo, stride=orbits), :] = make(o, slice(o * atoms + at, o * atoms + at + halo))

    @pl.when((parity[0] == 0) & ~near)
    def _():
        put(halo, lambda o, rows: base[rows, :])

    @pl.when((parity[0] == 0) & near)
    def _():
        put(0, lambda o, rows: base[rows, :] + 2.0 * got_x[o * halo : (o + 1) * halo, :].astype(F32))

    @pl.when((parity[0] != 0) & ~near)
    def _():
        full[...] = base[...] + 2.0 * times(cross, got_x[:edge_size, :])
        put(halo, lambda o, rows: full[rows, :])

    @pl.when((parity[0] != 0) & near)
    def _():
        put(0, lambda o, rows: full[rows, :])

    @pl.when(~near)
    def _():
        total = table[...]
        for one in got:
            total = total + get_table(one, edge_size)
        moments[...] = total


def per_device(probes, blocks, block_rows, block_cols, counts):
    atoms, orbits, width = probes.shape
    halo = atoms // 2
    size, edge_size = atoms * orbits, halo * orbits
    slots = blocks.shape[0]
    dims = (atoms, orbits, halo)
    turn = width == 128
    ring = lax.axis_size(RING)
    ride = ring == STEPS
    scale = 1.0 / (size * ring)
    parity = lax.axis_index("orb").astype(jnp.int32).reshape(1)
    between = [(i, (i + 1) % ring) for i in range(1, ring, 2)]
    between = between + [(b, a) for a, b in between]
    across = lambda x: lax.ppermute(x, RING, between)
    inside = lambda x: lax.ppermute(x, "orb", [(0, 1), (1, 0)])

    slot = jnp.arange(slots, dtype=jnp.int32)
    pair = jnp.where(slot < counts[0], block_cols * atoms + block_rows, -atoms)
    flat = blocks.transpose(1, 2, 0).reshape(orbits * orbits, slots)
    row_hot, cols = call(
        functools.partial(hot_body, atoms),
        (((atoms, slots), BF16), ((1, slots), jnp.int32)),
        pair,
        flops=AHEAD,
    )
    (crosst,) = call(
        functools.partial(cross_body, *dims),
        (((edge_size, size), BF16),),
        row_hot, cols, flat,
        flops=2 * orbits * orbits * slots * atoms * halo,
        scratch=[pltpu.VMEM((orbits // 2, orbits * (halo + PAD), 2 * atoms), F32)],
        limit=24,
    )
    whole, rounded, message = ((size, width), F32), ((size, width), BF16), ((edge_size, width), BF16)
    longer = ((edge_size + TAIL, width), BF16)
    riding = [ride and k >= HALF for k in range(STEPS)]
    far_rows = [edge_size + (TAIL if riding[k] else 0) + (0 if riding[k] and k % 2 else LONGER) for k in range(STEPS)]
    v, w, send_x, send_i = call(
        functools.partial(first_body, *dims, turn),
        (whole, rounded, ((far_rows[0], width), BF16), message),
        parity,
        (probes if turn else probes.transpose(1, 0, 2)).reshape(size, width),
        crosst,
        smem=1,
    )
    vectors, tables, got = [v], [], []
    for k in range(STEPS):
        got_x = across(send_x)
        if k > 0:
            tail = {HALF: "start", HALF + 2: "pass"}.get(k) if ride or k == HALF else None
            extra, outs = (), (whole, rounded, longer if tail and ride else message)[k == STEPS - 1 :]
            if k == HALF:
                extra, outs = (*(vectors[m] for m in operands_of(HALF)[:-1]), *tables), outs + (((ROWS, width), F32),)
            made = call(
                functools.partial(next_body, *dims, k - 1, tail, scale, ride),
                outs, parity, arrived, base, cross, crosst, send_x, *extra, smem=1,
            )
            if k < STEPS - 1:
                vectors.append(made[0])
            w, send_i = made[k < STEPS - 1 :][:2]
            if k == HALF:
                table = made[3]
        got_i = inside(send_i)
        if k == 0:
            own, cross, gram, local = call(
                functools.partial(own_body, *dims),
                (((size, size), BF16), ((size, edge_size), BF16), ((edge_size, edge_size), BF16), whole),
                row_hot, cols, flat, crosst, w, send_i,
                scratch=[pltpu.VMEM((orbits // 2, orbits * (atoms + PAD), 2 * atoms), F32)],
                limit=24,
            )
        else:
            dots = (((len(DOTS[k]), width), F32),) if k < HALF else ()
            local, *made = call(
                functools.partial(local_body, k),
                (whole,) + dots,
                own, w, *((vectors[m] for m in operands_of(k)) if k < HALF else ()),
            )
            tables = tables + made
        base, *pre = call(
            functools.partial(before_body, *dims, k),
            (whole, ((edge_size, width), F32))[: 2 - (k == STEPS - 1)],
            parity, got_i, local, vectors[max(k - 1, 0)], cross, crosst, smem=1,
        )
        arrived = got_x
        if k < STEPS - 1:
            tail = {HALF: "sum", HALF + 2: "pass"}.get(k) if ride else None
            extra = {"sum": (table, got_i), "pass": (got_i,)}[tail] if tail else ()
            (send_x,) = call(
                functools.partial(send_body, k, tail),
                (((far_rows[k + 1], width), BF16),),
                parity, got_x, *pre, gram, *extra, smem=1,
            )
        if ride and k >= HALF:
            got.append(got_i if k % 2 == 0 else got_x)
    operands = (parity, got_x, base, cross, table, *got)
    if turn:
        last, moments = pl.pallas_call(
            functools.partial(halves_body, *dims),
            grid=(2,),
            out_shape=(jax.ShapeDtypeStruct(*whole), jax.ShapeDtypeStruct((ROWS, width), F32)),
            in_specs=[SMEM] + [VMEM] * (len(operands) - 1),
            out_specs=(pl.BlockSpec((size // 2, width), lambda g: (1 - g, 0)), VMEM),
            scratch_shapes=[pltpu.VMEM((size, width), F32)],
            compiler_params=pltpu.CompilerParams(vmem_limit_bytes=16 << 20),
        )(*operands)
    else:
        last, moments = call(
            functools.partial(last_body, *dims, STEPS - 1, turn), (whole, ((ROWS, width), F32)), *operands, smem=1
        )
    last = last.reshape(atoms, orbits, width) if turn else last.reshape(orbits, atoms, width).transpose(1, 0, 2)
    return last, moments if ride else lax.psum(moments, RING)


def solution(mesh):
    in_specs = (
        P(("groups", "dom", "orb"), None, "probe"),
        P(("groups", "dom", "orb"), None, None),
        P(("groups", "dom", "orb")),
        P(("groups", "dom", "orb")),
        P(("groups", "dom", "orb")),
    )
    out_specs = (P(("groups", "dom", "orb"), None, "probe"), P("groups", "probe"))
    return jax.shard_map(
        per_device, mesh=mesh, in_specs=in_specs, out_specs=out_specs, check_vma=False
    )
```

```python
import functools

import jax
import jax.numpy as jnp
from jax import lax
from jax.experimental import pallas as pl
from jax.experimental.pallas import tpu as pltpu
from jax.sharding import PartitionSpec as P

STEPS = 8
HALF = STEPS // 2
RING = ("dom", "orb")
F32, BF16 = jnp.float32, jnp.bfloat16
VMEM = pl.BlockSpec(memory_space=pltpu.VMEM)
SMEM = pl.BlockSpec(memory_space=pltpu.SMEM)
NT = (((1,), (1,)), ((), ()))
AHEAD = 1_000_000_000
PAD = 8
ROWS = STEPS + 1
LONGER = 16
TAIL = -(-3 * ROWS // 16) * 16
DOTS = [[(0, n)] + [(m, n) for m in (n - 1, n) if m > 0 and HALF < m + n] for n in range(HALF + 1)]
DOTS[:2] = [[], DOTS[0] + DOTS[1]]


def operands_of(n):
    return sorted({m for pair in DOTS[n] for m in pair})


def call(body, outs, *operands, flops=0, scratch=(), smem=0, limit=16):
    size = sum(o.size * o.dtype.itemsize for o in operands)
    return pl.pallas_call(
        body,
        out_shape=tuple(jax.ShapeDtypeStruct(s, t) for s, t in outs),
        in_specs=[SMEM] * smem + [VMEM] * (len(operands) - smem),
        out_specs=(VMEM,) * len(outs),
        scratch_shapes=scratch,
        compiler_params=pltpu.CompilerParams(vmem_limit_bytes=limit << 20),
        cost_estimate=pl.CostEstimate(flops=flops, bytes_accessed=size, transcendentals=0) if flops else None,
    )(*operands)


def hot_body(atoms, pair, row_hot, col_ref):
    slots = pair.shape[0]
    pair_id = pair[...].reshape(1, slots)
    col_id = lax.div(pair_id, atoms)
    row_id = pair_id - col_id * atoms
    row_hot[...] = jnp.where(lax.broadcasted_iota(jnp.int32, (atoms, slots), 0) == row_id, 1.0, 0.0).astype(BF16)
    col_ref[...] = col_id


def place(atoms, orbits, first, total, row_hot, cols, blocks, target):
    col_id = cols[...]
    lanes = 2 * atoms
    lane = lax.broadcasted_iota(jnp.int32, (orbits, lanes), 1)

    def one(q, _):
        hot = []
        for n in range(4):
            here = jnp.where(col_id == first + 4 * q + n, 1.0, 0.0).astype(BF16)
            hot.append(row_hot[...] * here)
        hot = jnp.concatenate(hot, axis=0)
        tile = lax.dot_general(blocks[...], hot, NT, preferred_element_type=F32)
        for two in range(2):
            for i in range(0, orbits, 2):
                at = slice(two * lanes, (two + 1) * lanes)
                left = tile[i * orbits : (i + 1) * orbits, at]
                right = tile[(i + 1) * orbits : (i + 2) * orbits, at]
                low = jnp.where(lane < atoms, left, pltpu.roll(right, atoms, 1))
                high = jnp.where(lane < atoms, pltpu.roll(left, atoms, 1), right)
                col = 4 * q + 2 * two
                target[i // 2, pl.ds(col, orbits, stride=total + PAD), :] = low
                target[i // 2, pl.ds(col + 1, orbits, stride=total + PAD), :] = high
        return 0

    lax.fori_loop(0, total // 4, one, 0, unroll=total // 4)


def gather_rows(source, piece, total, orbitals):
    starts = [j * (total + PAD) for j in orbitals]
    return jnp.concatenate([source[piece, start : start + total, :] for start in starts], axis=0)


def cross_body(atoms, orbits, halo, row_hot, cols, blocks, crosst_ref, cross_f32):
    place(atoms, orbits, atoms, halo, row_hot, cols, blocks, cross_f32)
    lanes = 2 * atoms
    for p in range(orbits // 2):
        at = slice(p * lanes, (p + 1) * lanes)
        crosst_ref[:, at] = gather_rows(cross_f32, p, halo, range(orbits)).astype(BF16)


def own_body(atoms, orbits, halo, row_hot, cols, blocks, crosst, w, _, own_ref, cross_ref, gram_ref, local_ref, own_f32):
    place(atoms, orbits, 0, atoms, row_hot, cols, blocks, own_f32)
    gram_ref[...] = (2.0 * lax.dot_general(crosst[...], crosst[...], NT, preferred_element_type=F32)).astype(BF16)
    lanes = 2 * atoms
    for p in range(orbits // 2):
        at = slice(p * lanes, (p + 1) * lanes)
        cross_ref[at, :] = crosst[:, at].astype(F32).T.astype(BF16)
        turned = gather_rows(own_f32, p, atoms, range(orbits)).T
        parts = []
        for n in range(orbits // 2):
            other = gather_rows(own_f32, n, atoms, (2 * p, 2 * p + 1))
            parts.append((other + turned[:, n * lanes : (n + 1) * lanes]).astype(BF16))
        mine = jnp.concatenate(parts, axis=1)
        own_ref[at, :] = mine
        local_ref[at, :] = times(mine, w)


def put_edge(atoms, halo, w, out):
    for o in range(w.shape[0] // atoms):
        out[o * halo : (o + 1) * halo, :] = w[o * atoms : o * atoms + halo, :]


def blank(out, start):
    if start < out.shape[0]:
        out[start:, :] = jnp.zeros((out.shape[0] - start, out.shape[1]), out.dtype)


def times(left, right):
    return jnp.dot(left[...], right[...], preferred_element_type=F32)


def first_body(atoms, orbits, halo, turn, parity, probes, crosst, v_ref, w_ref, out_x, out_i):
    for o in range(orbits):
        rows = slice(o * atoms, (o + 1) * atoms)
        v = probes[pl.ds(o, atoms, stride=orbits), :] if turn else probes[rows, :]
        v_ref[rows, :] = v
        w_ref[rows, :] = v.astype(BF16)

    @pl.when(parity[0] == 0)
    def _():
        put_edge(atoms, halo, w_ref, out_x)
        out_i[...] = times(crosst, w_ref).astype(BF16)

    blank(out_x, orbits * halo)

    @pl.when(parity[0] != 0)
    def _():
        put_edge(atoms, halo, w_ref, out_i)
        out_x[: orbits * halo, :] = times(crosst, w_ref).astype(BF16)


def dots_of(n, refs):
    vectors = dict(zip(operands_of(n), refs))
    return [jnp.sum(vectors[a][...] * vectors[b][...], axis=0, keepdims=True) for a, b in DOTS[n]]


def local_body(k, own, w, *refs):
    refs[-1 if k >= HALF else -2][...] = times(own, w)
    if k < HALF:
        refs[-1][...] = jnp.concatenate(dots_of(k, refs), axis=0)


def table_of(scale, made, tables):
    dots = dict(zip(DOTS[HALF], made))
    for table, pairs in zip(tables, DOTS[1:]):
        dots.update({pair: table[n : n + 1, :] for n, pair in enumerate(pairs)})
    rows = [dots[0, n] for n in range(HALF + 1)]
    for n in range(HALF + 1, STEPS + 1):
        rows.append(2.0 * dots[n // 2, n - n // 2] - dots[0, n % 2])
    return jnp.concatenate(rows, axis=0) * scale


def put_table(table, out, start):
    pieces = []
    for _ in range(3):
        pieces.append(table.astype(BF16).astype(F32))
        table = table - pieces[-1]
    pieces.append(jnp.zeros((TAIL - 3 * ROWS, table.shape[1]), F32))
    out[start : start + TAIL, :] = jnp.concatenate(pieces, axis=0).astype(BF16)


def get_table(got, start):
    pieces = got[start : start + TAIL, :].astype(F32)
    return pieces[:ROWS] + (pieces[ROWS : 2 * ROWS] + pieces[2 * ROWS : 3 * ROWS])


def before_body(atoms, orbits, halo, k, parity, got_i, local, previous, cross, crosst, base_ref, pre_ref=None):
    edge_size = orbits * halo
    grown = lambda total, rows: total if k == 0 else 2.0 * total - previous[rows, :]

    @pl.when(parity[0] == 0)
    def _():
        total = local[...] + times(cross, got_i[:edge_size, :])
        base_ref[...] = grown(total, slice(None))
        if pre_ref is not None:
            put_edge(atoms, halo, base_ref, pre_ref)

    @pl.when(parity[0] != 0)
    def _():
        for o in range(orbits):
            near = slice(o * atoms, o * atoms + halo)
            far = slice(o * atoms + halo, (o + 1) * atoms)
            back = got_i[o * halo : (o + 1) * halo, :].astype(F32)
            base_ref[near, :] = grown(local[near, :] + back, near)
            base_ref[far, :] = grown(local[far, :], far)
        if pre_ref is not None:
            pre_ref[...] = times(crosst, base_ref[...].astype(BF16))


def send_body(k, tail, parity, got_x, pre, gram, *refs):
    out = refs[-1]
    edge_size = pre.shape[0]
    factor = 1.0 if k == 0 else 2.0

    @pl.when(parity[0] == 0)
    def _():
        out[:edge_size, :] = (pre[...] + factor * got_x[:edge_size, :].astype(F32)).astype(BF16)

    @pl.when(parity[0] != 0)
    def _():
        product = times(gram, got_x[:edge_size, :])
        out[:edge_size, :] = (pre[...] + (0.5 * product if k == 0 else product)).astype(BF16)

    if tail == "sum":
        table, got = refs[:-1]
        put_table(table[...] + get_table(got, edge_size), out, edge_size)
        blank(out, edge_size + TAIL)
    elif tail == "pass":
        out[edge_size : edge_size + TAIL, :] = refs[0][edge_size : edge_size + TAIL, :]
        blank(out, edge_size + TAIL)
    else:
        blank(out, edge_size)


def finish(atoms, orbits, halo, k, parity, got_x, base, cross, write):
    factor = 1.0 if k == 0 else 2.0

    @pl.when(parity[0] == 0)
    def _():
        for o in range(orbits):
            near = slice(o * atoms, o * atoms + halo)
            back = got_x[o * halo : (o + 1) * halo, :].astype(F32)
            write(o, 0, base[near, :] + factor * back)
            write(o, halo, base[o * atoms + halo : (o + 1) * atoms, :])

    @pl.when(parity[0] != 0)
    def _():
        total = base[...] + factor * times(cross, got_x[: orbits * halo, :])
        for o in range(orbits):
            write(o, 0, total[o * atoms : (o + 1) * atoms, :])


def next_body(atoms, orbits, halo, k, tail, scale, ride, parity, got_x, base, cross, crosst, _, *refs):
    keep = k < STEPS - 2
    outs = refs[len(refs) - 2 - keep - (tail == "start") :]
    (v_ref, w_ref, out) = outs[:3] if keep else (None, *outs)
    edge_size = orbits * halo

    def write(o, at, piece):
        rows = slice(o * atoms + at, o * atoms + at + piece.shape[0])
        if keep:
            v_ref[rows, :] = piece
        w_ref[rows, :] = piece.astype(BF16)

    finish(atoms, orbits, halo, k, parity, got_x, base, cross, write)

    @pl.when(parity[0] == 0)
    def _():
        out[:edge_size, :] = times(crosst, w_ref).astype(BF16)

    @pl.when(parity[0] != 0)
    def _():
        put_edge(atoms, halo, w_ref, out)

    if tail == "start":
        others = operands_of(HALF)[:-1]
        made = dots_of(HALF, refs[: len(others)] + (v_ref,))
        table = table_of(scale, made, refs[len(others) : len(others) + HALF - 1])
        outs[3][...] = table
        if ride:
            put_table(table, out, edge_size)
    elif tail == "pass":
        out[edge_size:, :] = got_x[edge_size : edge_size + TAIL, :]


def last_body(atoms, orbits, halo, k, turn, parity, got_x, base, cross, table, *refs):
    out, moments = refs[-2:]
    edge_size = orbits * halo

    def write(o, at, piece):
        rows = slice(o * atoms + at, o * atoms + at + piece.shape[0])
        out[pl.ds(at * orbits + o, piece.shape[0], stride=orbits) if turn else rows, :] = piece

    finish(atoms, orbits, halo, k, parity, got_x, base, cross, write)
    total = table[...]
    for got in refs[:-2]:
        total = total + get_table(got, edge_size)
    moments[...] = total


def per_device(probes, blocks, block_rows, block_cols, counts):
    atoms, orbits, width = probes.shape
    halo = atoms // 2
    size, edge_size = atoms * orbits, halo * orbits
    slots = blocks.shape[0]
    dims = (atoms, orbits, halo)
    turn = width == 128
    ring = lax.axis_size(RING)
    ride = ring == STEPS
    scale = 1.0 / (size * ring)
    parity = lax.axis_index("orb").astype(jnp.int32).reshape(1)
    between = [(i, (i + 1) % ring) for i in range(1, ring, 2)]
    between = between + [(b, a) for a, b in between]
    across = lambda x: lax.ppermute(x, RING, between)
    inside = lambda x: lax.ppermute(x, "orb", [(0, 1), (1, 0)])

    slot = jnp.arange(slots, dtype=jnp.int32)
    pair = jnp.where(slot < counts[0], block_cols * atoms + block_rows, -atoms)
    flat = blocks.transpose(1, 2, 0).reshape(orbits * orbits, slots)
    row_hot, cols = call(
        functools.partial(hot_body, atoms),
        (((atoms, slots), BF16), ((1, slots), jnp.int32)),
        pair,
        flops=AHEAD,
    )
    (crosst,) = call(
        functools.partial(cross_body, *dims),
        (((edge_size, size), BF16),),
        row_hot, cols, flat,
        flops=2 * orbits * orbits * slots * atoms * halo,
        scratch=[pltpu.VMEM((orbits // 2, orbits * (halo + PAD), 2 * atoms), F32)],
        limit=24,
    )
    whole, rounded, message = ((size, width), F32), ((size, width), BF16), ((edge_size, width), BF16)
    longer = ((edge_size + TAIL, width), BF16)
    riding = [ride and k >= HALF for k in range(STEPS)]
    far_rows = [edge_size + (TAIL if riding[k] else 0) + (0 if riding[k] and k % 2 else LONGER) for k in range(STEPS)]
    v, w, send_x, send_i = call(
        functools.partial(first_body, *dims, turn),
        (whole, rounded, ((far_rows[0], width), BF16), message),
        parity,
        (probes if turn else probes.transpose(1, 0, 2)).reshape(size, width),
        crosst,
        smem=1,
    )
    vectors, tables, got = [v], [], []
    for k in range(STEPS):
        got_x = across(send_x)
        if k > 0:
            tail = {HALF: "start", HALF + 2: "pass"}.get(k) if ride or k == HALF else None
            extra, outs = (), (whole, rounded, longer if tail and ride else message)[k == STEPS - 1 :]
            if k == HALF:
                extra, outs = (*(vectors[m] for m in operands_of(HALF)[:-1]), *tables), outs + (((ROWS, width), F32),)
            made = call(
                functools.partial(next_body, *dims, k - 1, tail, scale, ride),
                outs, parity, arrived, base, cross, crosst, send_x, *extra, smem=1,
            )
            if k < STEPS - 1:
                vectors.append(made[0])
            w, send_i = made[k < STEPS - 1 :][:2]
            if k == HALF:
                table = made[3]
        got_i = inside(send_i)
        if k == 0:
            own, cross, gram, local = call(
                functools.partial(own_body, *dims),
                (((size, size), BF16), ((size, edge_size), BF16), ((edge_size, edge_size), BF16), whole),
                row_hot, cols, flat, crosst, w, send_i,
                scratch=[pltpu.VMEM((orbits // 2, orbits * (atoms + PAD), 2 * atoms), F32)],
                limit=24,
            )
        else:
            dots = (((len(DOTS[k]), width), F32),) if k < HALF else ()
            local, *made = call(
                functools.partial(local_body, k),
                (whole,) + dots,
                own, w, *((vectors[m] for m in operands_of(k)) if k < HALF else ()),
            )
            tables = tables + made
        base, *pre = call(
            functools.partial(before_body, *dims, k),
            (whole, ((edge_size, width), F32))[: 2 - (k == STEPS - 1)],
            parity, got_i, local, vectors[max(k - 1, 0)], cross, crosst, smem=1,
        )
        arrived = got_x
        if k < STEPS - 1:
            tail = {HALF: "sum", HALF + 2: "pass"}.get(k) if ride else None
            extra = {"sum": (table, got_i), "pass": (got_i,)}[tail] if tail else ()
            (send_x,) = call(
                functools.partial(send_body, k, tail),
                (((far_rows[k + 1], width), BF16),),
                parity, got_x, *pre, gram, *extra, smem=1,
            )
        if ride and k >= HALF:
            got.append(got_i if k % 2 == 0 else got_x)
    last, moments = call(
        functools.partial(last_body, *dims, STEPS - 1, turn),
        (whole, ((STEPS + 1, width), F32)),
        parity, got_x, base, cross, table, *got, smem=1,
    )
    last = last.reshape(atoms, orbits, width) if turn else last.reshape(orbits, atoms, width).transpose(1, 0, 2)
    return last, moments if ride else lax.psum(moments, RING)


def solution(mesh):
    in_specs = (
        P(("groups", "dom", "orb"), None, "probe"),
        P(("groups", "dom", "orb"), None, None),
        P(("groups", "dom", "orb")),
        P(("groups", "dom", "orb")),
        P(("groups", "dom", "orb")),
    )
    out_specs = (P(("groups", "dom", "orb"), None, "probe"), P("groups", "probe"))
    return jax.shard_map(
        per_device, mesh=mesh, in_specs=in_specs, out_specs=out_specs, check_vma=False
    )
```
